32 devices in a mesh: dp: 16 (over z, y, x), tensor: 2 (over core).
Axes of the slice: x: 2, y: 2, z: 4, core: 2. Of those that a mesh axis runs over, the one named last changes fastest.
Arguments:
- tokens: bfloat16 [6144, 576], P(('dp', 'tensor')), may hold values from -6 to 6
- w_attn: bfloat16 [2, 1536, 576], replicated, as said below
- attn_gain: float32 [2, 576], replicated, may hold values from 0.5 to 1.5
- w_gate: bfloat16 [2, 1536, 576], P(None, 'tensor'), may hold values from -0.25 to 0.25
- w_up: bfloat16 [2, 1536, 576], P(None, 'tensor'), may hold values from -0.25 to 0.25
- w_down: bfloat16 [2, 1536, 576], P(None, 'tensor'), may hold values from -0.15625 to 0.15625
- mlp_gain: float32 [2, 576], replicated, may hold values from 0.5 to 1.5
- seq_lengths: int32 [4], replicated, may hold values from 1024 to 2048, as said below
- cotangent: bfloat16 [6144, 576], P(('dp', 'tensor')), may hold values from -6 to 6
Outputs:
- out_act: float32 [6144, 576], P(('dp', 'tensor'))
- in_grad: float32 [6144, 576], P(('dp', 'tensor'))
- grad_attn: float32 [2, 1536, 576], P(None, ('dp', 'tensor'))
- grad_attn_gain: float32 [2, 576], replicated
- grad_gate: float32 [2, 1536, 576], P(None, ('tensor', 'dp'))
- grad_up: float32 [2, 1536, 576], P(None, ('tensor', 'dp'))
- grad_down: float32 [2, 1536, 576], P(None, ('tensor', 'dp'))
- grad_mlp_gain: float32 [2, 576], replicated
The draws below stay inside these ranges and needn't reach their ends.
Inputs may be any that keep to these rules, and one draw needn't show every extreme that they name: `seq_lengths`: the lengths sum to 6144; one of them is exactly 2048. `w_attn`: independent entries of mean zero.
All inputs are finite; a program needn't handle non-finite values.
Results may differ from the reference program's by a relative error of at most 0.018.
Values may be sent and summed in bfloat16 or wider, within the bound.
A program may use at most 192 MiB of HBM per device.

```python
import math
import jax
import jax.numpy as jnp
from jax import lax

D = 576
H = 9
KV = 3
HD = 64
FF = 1536
LAYERS = 2
L_MIN = 1024
L_MAX = 2048
TOKENS = 6144
NSEQ = 4
ATT_ROWS = 1536


def draw_w_attn(key, part):
    key = jax.random.fold_in(key, 7)
    noise = jax.random.normal(key, (LAYERS, ATT_ROWS, D), jnp.float32)
    row_ids = jnp.arange(ATT_ROWS)
    out_scale = D ** (-0.5) * L_MIN ** 0.5 / 4.0
    scales = jnp.where(row_ids < (H + 2 * KV) * HD, D ** (-0.5), out_scale)
    return (noise * scales[None, :, None]).astype(jnp.bfloat16)


def draw_seq_lengths(key, part):
    key = jax.random.fold_in(key, 11)
    weight_key, order_key = jax.random.split(key)
    extra_total = TOKENS - L_MAX - (NSEQ - 1) * L_MIN
    shares = jax.random.randint(weight_key, (NSEQ - 1,), 500, 1001).astype(jnp.int32)
    share_sum = jnp.sum(shares).astype(jnp.int32)
    extras = extra_total * shares // share_sum
    leftover = extra_total - jnp.sum(extras)
    extras = extras + (jnp.arange(NSEQ - 1, dtype=jnp.int32) < leftover).astype(jnp.int32)
    lengths = jnp.concatenate([jnp.full((1,), L_MAX, jnp.int32), (L_MIN + extras).astype(jnp.int32)], axis=0)
    order = jax.random.permutation(order_key, NSEQ)
    return lengths[order].astype(jnp.int32)


def levels(stream_key, shape, pieces, least, high):
    def one(axis_at, parts):
        heights = jax.random.uniform(jax.random.fold_in(jax.random.fold_in(stream_key, 6), axis_at), (parts,), jnp.float32, least / len(pieces), high / len(pieces))
        return jnp.repeat(jnp.exp(heights), shape[axis_at] // parts).reshape((-1,) + (1,) * (len(shape) - axis_at - 1))

    level = one(*pieces[0])
    for cut in pieces[1:]:
        level = level * one(*cut)
    return level


def centred(own_key, shape, width, reach, pieces=(), kind=jnp.bfloat16):
    values = jax.random.normal(own_key, shape, jnp.float32) * width
    if len(pieces) > 0:
        values = levels(own_key, shape, pieces, -0.22, 0.18) * values
    return jnp.clip(values, min=-reach, max=reach).astype(kind)


def setup_inputs(seed: int = 0) -> dict:
    seeds = jax.random.split(jax.random.key(seed), 10)
    return {
        "tokens": centred(seeds[0], (TOKENS, D), 1.0, 6.0, ((0, 32),)),
        "w_attn": draw_w_attn(jax.random.fold_in(seeds[9], 71), 0),
        "attn_gain": jnp.clip(1.0 + 0.1 * jax.random.normal(seeds[2], (LAYERS, D), jnp.float32), 0.5, 1.5),
        "w_gate": centred(seeds[3], (LAYERS, FF, D), D ** -0.5, 0.25, ((1, 2),)),
        "w_up": centred(seeds[4], (LAYERS, FF, D), D ** -0.5, 0.25, ((1, 2),)),
        "w_down": centred(seeds[5], (LAYERS, FF, D), FF ** -0.5, 0.15625, ((1, 2),)),
        "mlp_gain": jnp.clip(1.0 + 0.1 * jax.random.normal(seeds[6], (LAYERS, D), jnp.float32), 0.5, 1.5),
        "seq_lengths": draw_seq_lengths(jax.random.fold_in(seeds[9], 71), 0),
        "cotangent": centred(seeds[8], (TOKENS, D), 1.0, 6.0, ((0, 32),)),
    }


@jax.custom_vjp
def low(v):
    return lax.optimization_barrier(v.astype(jnp.bfloat16)).astype(jnp.float32)

@jax.custom_vjp
def low_back(v):
    return v

def low_keep(v):
    return (low(v), None)

def low_pass(kept, grad):
    return (grad,)

def back_keep(v):
    return (v, None)

def back_low(kept, grad):
    return (low(grad),)
low.defvjp(low_keep, low_pass)
low_back.defvjp(back_keep, back_low)
EPSILON = 1e-05
ROPE_BASE = 100000.0
MASKED = -1e+30
PRECISE = lax.Precision.HIGHEST

def sequence_start(places, starts):
    reached = starts[None, :] <= places[:, None]
    return lax.optimization_barrier(jnp.max(jnp.where(reached, starts[None, :], -1), axis=1))

def rope_tables(relative):
    half_size = HD // 2
    frequencies = jnp.power(ROPE_BASE, -2.0 * jnp.arange(half_size, dtype=jnp.float32) / HD)
    angles = relative.astype(jnp.float32)[:, None] * frequencies[None, :]
    return (jnp.cos(angles)[:, None, :], jnp.sin(angles)[:, None, :])

def rotate(values, cosines, sines):
    half_size = values.shape[-1] // 2
    first_half = values[..., :half_size]
    second_half = values[..., half_size:]
    return jnp.concatenate([first_half * cosines - second_half * sines, second_half * cosines + first_half * sines], axis=-1)

def normalize(values, gain_vec):
    inverse = lax.rsqrt(lax.optimization_barrier(jnp.mean(values * values, axis=-1, keepdims=True)) + EPSILON)
    return values * inverse * gain_vec

def attention(queries, key_rows, values, starts):
    query_block = math.gcd(TOKENS, 512)
    key_span = L_MAX + query_block
    groups = H // KV
    pad_keys = jnp.concatenate([jnp.zeros((L_MAX, KV, HD), key_rows.dtype), key_rows], axis=0)
    pad_values = jnp.concatenate([jnp.zeros((L_MAX, KV, HD), values.dtype), values], axis=0)
    places = jnp.arange(TOKENS, dtype=jnp.int32)
    key_places = jnp.arange(TOKENS + L_MAX, dtype=jnp.int32) - L_MAX
    query_starts = sequence_start(places, starts)
    key_starts = sequence_start(key_places, starts)

    def one_block(block_index):
        first_row = (block_index * query_block).astype(jnp.int32)
        query_rows = lax.dynamic_slice_in_dim(queries, first_row, query_block, 0).reshape(query_block, KV, groups, HD)
        block_keys = lax.dynamic_slice_in_dim(pad_keys, first_row, key_span, 0)
        value_rows = lax.dynamic_slice_in_dim(pad_values, first_row, key_span, 0)
        query_here = lax.dynamic_slice_in_dim(places, first_row, query_block, 0)
        start_here = lax.dynamic_slice_in_dim(query_starts, first_row, query_block, 0)
        key_here = lax.dynamic_slice_in_dim(key_places, first_row, key_span, 0)
        kstart_here = lax.dynamic_slice_in_dim(key_starts, first_row, key_span, 0)
        allowed = (kstart_here[None, :] == start_here[:, None]) & (key_here[None, :] <= query_here[:, None])
        scores = low_back(0.125 * jnp.einsum('tkgd,skd->kgts', query_rows, block_keys, precision=PRECISE))
        scores = jnp.where(allowed[None, None], scores, MASKED)
        log_total = jax.nn.logsumexp(scores, axis=-1, keepdims=True)
        weights = low(jnp.exp(scores - log_total))
        mixed_rows = jnp.einsum('kgts,skd->tkgd', weights, value_rows, precision=PRECISE)
        return mixed_rows.reshape(query_block, H * HD)
    blocks = lax.map(jax.checkpoint(one_block), jnp.arange(TOKENS // query_block, dtype=jnp.int32))
    return blocks.reshape(TOKENS, H * HD)

def one_layer(stream, attn_w, gain_a, gate_w, up_w, down_w, gain_m, starts, cosines, sines):
    qkv_rows = (H + 2 * KV) * HD
    normed = low(normalize(stream, gain_a))
    projected = jnp.dot(normed, attn_w[:qkv_rows].T, precision=PRECISE, preferred_element_type=jnp.float32)
    q_lin = low_back(projected[:, :H * HD]).reshape(TOKENS, H, HD)
    k_lin = low_back(projected[:, H * HD:(H + KV) * HD]).reshape(TOKENS, KV, HD)
    v_lin = low_back(projected[:, (H + KV) * HD:]).reshape(TOKENS, KV, HD)
    queries = low(rotate(q_lin, cosines, sines))
    key_rows = low(rotate(k_lin, cosines, sines))
    values = low(v_lin)
    mixed_heads = low(low_back(attention(queries, key_rows, values, starts)))
    branch = low_back(jnp.dot(mixed_heads, attn_w[qkv_rows:].T, precision=PRECISE, preferred_element_type=jnp.float32))
    middle = stream + branch
    normed_m = low(normalize(middle, gain_m))
    gate_pre = low_back(jnp.dot(normed_m, gate_w.T, precision=PRECISE, preferred_element_type=jnp.float32))
    up_pre = low_back(jnp.dot(normed_m, up_w.T, precision=PRECISE, preferred_element_type=jnp.float32))
    hidden = low(jax.nn.silu(gate_pre) * up_pre)
    return middle + low_back(jnp.dot(hidden, down_w, precision=PRECISE, preferred_element_type=jnp.float32))

def reference(tokens, w_attn, attn_gain, w_gate, w_up, w_down, mlp_gain, seq_lengths, cotangent):
    flat_lengths = seq_lengths.reshape(-1).astype(jnp.int32)
    seq_ends = jnp.cumsum(flat_lengths).astype(jnp.int32)
    starts = (seq_ends - flat_lengths).astype(jnp.int32)
    places = jnp.arange(TOKENS, dtype=jnp.int32)
    cosines, sines = rope_tables(places - sequence_start(places, starts))

    def forward(stream, attn_all, gain_a_all, gate_all, up_all, down_all, gain_m_all):
        for layer_index in range(LAYERS):
            stream = one_layer(stream, attn_all[layer_index], gain_a_all[layer_index], gate_all[layer_index], up_all[layer_index], down_all[layer_index], gain_m_all[layer_index], starts, cosines, sines)
        return stream
    floats = (tokens.astype(jnp.float32), w_attn.astype(jnp.float32), attn_gain.astype(jnp.float32), w_gate.astype(jnp.float32), w_up.astype(jnp.float32), w_down.astype(jnp.float32), mlp_gain.astype(jnp.float32))
    result, pullback = jax.vjp(forward, *floats)
    gradients = pullback(cotangent.astype(jnp.float32))
    return (result, gradients[0], gradients[1], gradients[2], gradients[3], gradients[4], gradients[5], gradients[6])
```

```python
import functools

import jax
import jax.numpy as jnp
from jax import lax
from jax.experimental import pallas as pl
from jax.experimental.pallas import tpu as pltpu
from jax.sharding import PartitionSpec as P

H = 9
KV = 3
GROUPS = H // KV
HD = 64
TILE = 2 * HD
L_MAX = 2048

EPSILON = 1e-05
ROPE_BASE = 100000.0
MASKED = -1e30
MESH = pl.DeviceIdType.MESH
AXES = ("dp", "tensor")
VMEM_LIMIT = 56 * 1024 * 1024


def rows_by_rows(left, right):
    return lax.dot_general(
        left, right, (((1,), (1,)), ((), ())), preferred_element_type=jnp.float32
    )


def cols_by_cols(left, right):
    return lax.dot_general(
        left, right, (((0,), (0,)), ((), ())), preferred_element_type=jnp.float32
    )


def plain_dot(left, right):
    return jnp.dot(left, right, preferred_element_type=jnp.float32)


def sequence_start(places, starts):
    reached = starts[None, :] <= places[:, None]
    return jnp.max(jnp.where(reached, starts[None, :], -1), axis=1)


def rms_parts(values):
    inverse = lax.rsqrt(jnp.mean(values * values, axis=-1, keepdims=True) + EPSILON)
    return (values * inverse, inverse)


def norm_back(grad_out, ratio, inverse, gain_vec):
    scaled = grad_out * gain_vec
    input_grad = inverse * (scaled - ratio * jnp.mean(scaled * ratio, axis=-1, keepdims=True))
    return (input_grad, jnp.sum(grad_out * ratio, axis=0, keepdims=True))


def swap_halves(values):
    lane = lax.broadcasted_iota(jnp.int32, values.shape, 1)
    return jnp.where(
        lane < HD // 2,
        pltpu.roll(values, TILE - HD // 2, 1),
        pltpu.roll(values, HD // 2, 1),
    )


def call(kernel, out_shape, scratch=(), **params):
    return pl.pallas_call(
        kernel,
        out_shape=out_shape,
        scratch_shapes=list(scratch),
        compiler_params=pltpu.CompilerParams(vmem_limit_bytes=VMEM_LIMIT, **params),
    )


def project_kernel(x_ref, gain_ref, w_ref, cq_ref, ckv_ref, sn_ref, q_ref, kv_ref, a_ref):
    own = x_ref.shape[0]
    ratio, _ = rms_parts(x_ref[...])
    normed = (ratio * gain_ref[...]).astype(jnp.bfloat16)
    a_ref[...] = normed
    sines = sn_ref[...]
    for head in range(H + KV):
        lin = rows_by_rows(normed, w_ref[head * TILE : (head + 1) * TILE, :])
        cosines = cq_ref[...] if head < H else ckv_ref[...]
        turned = (lin * cosines + swap_halves(lin) * sines).astype(jnp.bfloat16)
        if head < H:
            rows = slice((head % GROUPS) * own, (head % GROUPS + 1) * own)
            q_ref[head // GROUPS, rows, :] = turned * jnp.bfloat16(0.125)
        else:
            kv_ref[:, (head - H) * TILE : (head - H + 1) * TILE] = turned


def mesh_id(index, pair):
    return {"dp": lax.div(index, pair), "tensor": lax.rem(index, pair)}


def greet(me, count, reach, step):
    barrier = pltpu.get_barrier_semaphore()
    pair = lax.axis_size("tensor")
    for by in range(1, reach + 1):
        sender = me + step * by

        @pl.when((sender >= 0) & (sender < count))
        def _():
            pl.semaphore_signal(
                barrier, inc=1, device_id=mesh_id(sender, pair), device_id_type=MESH
            )

    copied_to = jnp.minimum(count - 1 - me if step < 0 else me, reach)

    @pl.when(copied_to > 0)
    def _():
        pl.semaphore_wait(barrier, copied_to)


def fetch_kernel(count, reach, own_ref, window_ref, send_sem, recv_sem):
    pair = lax.axis_size("tensor")
    me = lax.axis_index("dp") * pair + lax.axis_index("tensor")
    greet(me, count, reach, -1)

    def send(by):
        return pltpu.make_async_remote_copy(
            src_ref=own_ref,
            dst_ref=window_ref.at[reach - by],
            send_sem=send_sem.at[by - 1],
            recv_sem=recv_sem.at[by - 1],
            device_id=mesh_id(me + by, pair),
            device_id_type=MESH,
        )

    for by in range(1, reach + 1):

        @pl.when(me + by < count)
        def _():
            send(by).start()

    window_ref[reach] = own_ref[...]
    for by in range(1, reach + 1):

        @pl.when(me - by < 0)
        def _():
            window_ref[reach - by] = jnp.zeros(own_ref.shape, own_ref.dtype)

    for by in range(1, reach + 1):

        @pl.when(me - by >= 0)
        def _():
            send(by).wait_recv()

        @pl.when(me + by < count)
        def _():
            send(by).wait_send()


def return_kernel(count, reach, grads_ref, sum_ref, held, send_sem, recv_sem):
    pair = lax.axis_size("tensor")
    me = lax.axis_index("dp") * pair + lax.axis_index("tensor")
    greet(me, count, reach, 1)

    def send(by):
        return pltpu.make_async_remote_copy(
            src_ref=grads_ref.at[reach - by],
            dst_ref=held.at[by - 1],
            send_sem=send_sem.at[by - 1],
            recv_sem=recv_sem.at[by - 1],
            device_id=mesh_id(me - by, pair),
            device_id_type=MESH,
        )

    for by in range(reach, 0, -1):

        @pl.when(me - by >= 0)
        def _():
            send(by).start()

    sum_ref[...] = grads_ref[reach].astype(jnp.float32)
    for by in range(1, reach + 1):

        @pl.when(me + by < count)
        def _():
            send(by).wait_recv()
            sum_ref[...] += held[by - 1].astype(jnp.float32)

        @pl.when(me - by >= 0)
        def _():
            send(by).wait_send()


def allowed_pairs(chunk, rows, low_ref, high_ref):
    place = chunk * rows + lax.broadcasted_iota(jnp.int32, (rows, low_ref.shape[1]), 0)
    return (place >= low_ref[...]) & (place <= high_ref[...])


def attend_kernel(
    chunk_rows,
    q_ref,
    win_ref,
    low_ref,
    high_ref,
    x_ref,
    wo_ref,
    gain_ref,
    wg_ref,
    wu_ref,
    wd_ref,
    x_out_ref,
    mid_ref,
    m_ref,
    gate_ref,
    up_ref,
    hidden_ref,
    o_ref,
    lse_ref,
    acc_ref,
    top_ref,
    total_ref,
):
    own = x_ref.shape[0]
    chunks = win_ref.shape[0] // chunk_rows
    acc_ref[...] = jnp.zeros_like(acc_ref)
    total_ref[...] = jnp.zeros_like(total_ref)
    top_ref[...] = jnp.full_like(top_ref, MASKED)

    def step(chunk, unused):
        allowed = allowed_pairs(chunk, chunk_rows, low_ref, high_ref)
        start = pl.multiple_of(chunk * chunk_rows, chunk_rows)
        for j in range(KV):
            tile = win_ref[pl.ds(start, chunk_rows), j * TILE : (j + 1) * TILE]
            scores = jnp.where(allowed, rows_by_rows(tile, q_ref[j]), MASKED)
            highest = top_ref[j]
            newest = jnp.maximum(highest, jnp.max(scores, axis=0, keepdims=True))
            terms = jnp.exp(scores - newest)
            decay = jnp.exp(highest - newest)
            top_ref[j] = newest
            total_ref[j] = total_ref[j] * decay + jnp.sum(terms, axis=0, keepdims=True)
            acc_ref[j] = acc_ref[j] * decay + cols_by_cols(tile, terms.astype(jnp.bfloat16))
        return unused

    lax.fori_loop(0, chunks, step, 0)
    middle = x_ref[...]
    for j in range(KV):
        lse_ref[j] = top_ref[j] + jnp.log(total_ref[j])
        mixed = (acc_ref[j] / total_ref[j]).T
        o_ref[j] = mixed
        low = mixed.astype(jnp.bfloat16)
        for g in range(GROUPS):
            middle = middle + plain_dot(low[g * own : (g + 1) * own], wo_ref[j * GROUPS + g])
    mid_ref[...] = middle
    ratio, _ = rms_parts(middle)
    normed = (ratio * gain_ref[...]).astype(jnp.bfloat16)
    m_ref[...] = normed
    gate = rows_by_rows(normed, wg_ref[...])
    up = rows_by_rows(normed, wu_ref[...])
    gate_ref[...] = gate
    up_ref[...] = up
    hidden = (gate * jax.nn.sigmoid(gate) * up).astype(jnp.bfloat16)
    hidden_ref[...] = hidden
    x_out_ref[...] = middle + plain_dot(hidden, wd_ref[...])


def mlp_back_kernel(
    gx_ref,
    mid_ref,
    gate_ref,
    up_ref,
    gain_ref,
    wg_ref,
    wu_ref,
    wd_ref,
    gy_ref,
    ggate_ref,
    gup_ref,
    gmid_ref,
    go_ref,
    ggain_ref,
):
    gx = gx_ref[...].astype(jnp.float32)
    gy = gx.astype(jnp.bfloat16)
    gy_ref[...] = gy
    gh = rows_by_rows(gy, wd_ref[...])
    gate = gate_ref[...]
    sig = jax.nn.sigmoid(gate)
    ggate = (gh * up_ref[...] * sig * (1.0 + gate * (1.0 - sig))).astype(jnp.bfloat16)
    gup = (gh * gate * sig).astype(jnp.bfloat16)
    ggate_ref[...] = ggate
    gup_ref[...] = gup
    gm = plain_dot(ggate, wg_ref[...]) + plain_dot(gup, wu_ref[...])
    ratio, inverse = rms_parts(mid_ref[...])
    back, ggain = norm_back(gm, ratio, inverse, gain_ref[...])
    ggain_ref[...] = ggain
    gmid = gx + back
    gmid_ref[...] = gmid
    go_ref[...] = gmid.astype(jnp.bfloat16)


def attend_back_kernel(
    chunk_rows,
    go_ref,
    wo_ref,
    q_ref,
    win_ref,
    low_ref,
    high_ref,
    o_ref,
    lse_ref,
    gq_ref,
    gwin_ref,
    grad_ref,
    delta_ref,
    acc_ref,
):
    own = go_ref.shape[0]
    chunks = win_ref.shape[0] // chunk_rows
    go = go_ref[...]
    lane = lax.broadcasted_iota(jnp.int32, (GROUPS * own, TILE), 1)
    for j in range(KV):
        for g in range(GROUPS):
            grad_ref[j, g * own : (g + 1) * own, :] = rows_by_rows(
                go, wo_ref[j * GROUPS + g]
            ).astype(jnp.bfloat16)
        product = jnp.where(lane >= HD, grad_ref[j].astype(jnp.float32) * o_ref[j], 0.0)
        delta_ref[j] = jnp.sum(product.T, axis=0, keepdims=True)
    acc_ref[...] = jnp.zeros_like(acc_ref)

    def step(chunk, unused):
        allowed = allowed_pairs(chunk, chunk_rows, low_ref, high_ref)
        start = pl.multiple_of(chunk * chunk_rows, chunk_rows)
        for j in range(KV):
            tile = win_ref[pl.ds(start, chunk_rows), j * TILE : (j + 1) * TILE]
            queries = q_ref[j]
            grads = grad_ref[j]
            scores = rows_by_rows(tile, queries) - lse_ref[j]
            weights = jnp.exp(jnp.where(allowed, scores, MASKED))
            slopes = rows_by_rows(tile, grads) - delta_ref[j]
            score_grads = (weights * slopes).astype(jnp.bfloat16)
            acc_ref[j] += cols_by_cols(tile, score_grads)
            both = plain_dot(score_grads, queries) + plain_dot(
                weights.astype(jnp.bfloat16), grads
            )
            gwin_ref[pl.ds(start, chunk_rows), j * TILE : (j + 1) * TILE] = both.astype(
                jnp.bfloat16
            )
        return unused

    lax.fori_loop(0, chunks, step, 0)
    for j in range(KV):
        gq_ref[j] = (0.125 * acc_ref[j]).T


def project_back_kernel(
    gq_ref, gkv_ref, cq_ref, ckv_ref, sn_ref, w_ref, x_ref, gain_ref, gmid_ref, gqkv_ref, gx_ref, ggain_ref
):
    own = x_ref.shape[0]
    sines = -sn_ref[...]
    for head in range(H + KV):
        if head < H:
            rows = slice((head % GROUPS) * own, (head % GROUPS + 1) * own)
            lin = gq_ref[head // GROUPS, rows, :]
            cosines = cq_ref[...]
        else:
            lin = gkv_ref[:, (head - H) * TILE : (head - H + 1) * TILE]
            cosines = ckv_ref[...]
        turned = (lin * cosines + swap_halves(lin) * sines).astype(jnp.bfloat16)
        gqkv_ref[:, head * TILE : (head + 1) * TILE] = turned
    grad_normed = plain_dot(gqkv_ref[...], w_ref[...])
    ratio, inverse = rms_parts(x_ref[...])
    back, ggain = norm_back(grad_normed, ratio, inverse, gain_ref[...])
    ggain_ref[...] = ggain
    gx_ref[...] = gmid_ref[...] + back


def body(tokens, w_attn, attn_gain, w_gate, w_up, w_down, mlp_gain, seq_lengths, cotangent):
    own, width = tokens.shape
    layers = w_attn.shape[0]
    count = lax.axis_size("dp") * lax.axis_size("tensor")
    qkv_rows = (H + 2 * KV) * HD
    reach = min((L_MAX + own - 2) // own, count - 1)
    window_rows = (reach + 1) * own
    chunk_rows = 2 * own if (reach + 1) % 2 == 0 else own
    tiles = (H + KV) * TILE
    f32, bf16 = jnp.float32, jnp.bfloat16
    shape = jax.ShapeDtypeStruct

    seq_ends = jnp.cumsum(seq_lengths)
    starts = seq_ends - seq_lengths
    first_place = lax.axis_index(AXES) * own
    places = first_place + jnp.arange(own, dtype=jnp.int32)
    begin = sequence_start(places, starts)
    first_key = first_place - reach * own
    low = jnp.tile(begin - first_key, GROUPS)[None, :]
    high = jnp.tile(places - first_key, GROUPS)[None, :]
    frequencies = jnp.power(ROPE_BASE, -2.0 * jnp.arange(HD // 2, dtype=f32) / HD)
    angles = (places - begin).astype(f32)[:, None] * frequencies[None, :]
    cosines, sines = jnp.cos(angles), jnp.sin(angles)
    zeros, ones = jnp.zeros((own, HD), f32), jnp.ones((own, HD), f32)
    cos_q = jnp.concatenate([cosines, cosines, zeros], axis=1)
    cos_kv = jnp.concatenate([cosines, cosines, ones], axis=1)
    sin_all = jnp.concatenate([-sines, sines, zeros], axis=1)

    gate_all = lax.all_gather(w_gate, "tensor", axis=1, tiled=True)
    up_all = lax.all_gather(w_up, "tensor", axis=1, tiled=True)
    down_all = lax.all_gather(w_down, "tensor", axis=1, tiled=True)
    q_rows = w_attn[:, : H * HD].reshape(layers, H, HD, width)
    k_rows = w_attn[:, H * HD : (H + KV) * HD].reshape(layers, KV, HD, width)
    v_rows = w_attn[:, (H + KV) * HD : qkv_rows].reshape(layers, KV, HD, width)
    w_in = jnp.concatenate(
        [
            jnp.pad(q_rows, ((0, 0), (0, 0), (0, HD), (0, 0))),
            jnp.concatenate([k_rows, v_rows], axis=2),
        ],
        axis=1,
    ).reshape(layers, tiles, width)
    w_out = jnp.pad(
        jnp.swapaxes(w_attn[:, qkv_rows:], 1, 2).reshape(layers, H, HD, width),
        ((0, 0), (0, 0), (HD, 0), (0, 0)),
    )

    stream = tokens.astype(f32)
    stored = []
    for layer in range(layers):
        queries, kv_own, normed = call(
            project_kernel,
            (
                shape((KV, GROUPS * own, TILE), bf16),
                shape((own, KV * TILE), bf16),
                shape((own, width), bf16),
            ),
        )(stream, attn_gain[layer][None], w_in[layer], cos_q, cos_kv, sin_all)
        window = call(
            functools.partial(fetch_kernel, count, reach),
            shape((reach + 1, own, KV * TILE), bf16),
            [pltpu.SemaphoreType.DMA((reach,)), pltpu.SemaphoreType.DMA((reach,))],
            collective_id=0,
            has_side_effects=True,
        )(kv_own).reshape(window_rows, KV * TILE)
        hidden_rows = gate_all.shape[1]
        x_out, middle, normed_m, gate, up, hidden, mixed, lse = call(
            functools.partial(attend_kernel, chunk_rows),
            (
                shape((own, width), f32),
                shape((own, width), f32),
                shape((own, width), bf16),
                shape((own, hidden_rows), f32),
                shape((own, hidden_rows), f32),
                shape((own, hidden_rows), bf16),
                shape((KV, GROUPS * own, TILE), f32),
                shape((KV, 1, GROUPS * own), f32),
            ),
            [
                pltpu.VMEM((KV, TILE, GROUPS * own), f32),
                pltpu.VMEM((KV, 1, GROUPS * own), f32),
                pltpu.VMEM((KV, 1, GROUPS * own), f32),
            ],
        )(
            queries,
            window,
            low,
            high,
            stream,
            w_out[layer],
            mlp_gain[layer][None],
            gate_all[layer],
            up_all[layer],
            down_all[layer],
        )
        stored.append((stream, queries, normed, window, middle, normed_m, gate, up, hidden, mixed, lse))
        stream = x_out

    upstream = cotangent
    gains = []
    sums = []
    for layer in reversed(range(layers)):
        x_in, queries, normed, window, middle, normed_m, gate, up, hidden, mixed, lse = stored[layer]
        hidden_rows = gate_all.shape[1]
        gy, ggate, gup, gmid, go, gain_m = call(
            mlp_back_kernel,
            (
                shape((own, width), bf16),
                shape((own, hidden_rows), bf16),
                shape((own, hidden_rows), bf16),
                shape((own, width), f32),
                shape((own, width), bf16),
                shape((1, width), f32),
            ),
        )(
            upstream,
            middle,
            gate,
            up,
            mlp_gain[layer][None],
            gate_all[layer],
            up_all[layer],
            down_all[layer],
        )
        heads = jnp.transpose(
            mixed.reshape(H, own, TILE)[:, :, HD:].astype(bf16), (1, 0, 2)
        ).reshape(own, H * HD)
        gq, gwin = call(
            functools.partial(attend_back_kernel, chunk_rows),
            (
                shape((KV, GROUPS * own, TILE), f32),
                shape((window_rows, KV * TILE), bf16),
            ),
            [
                pltpu.VMEM((KV, GROUPS * own, TILE), bf16),
                pltpu.VMEM((KV, 1, GROUPS * own), f32),
                pltpu.VMEM((KV, TILE, GROUPS * own), f32),
            ],
        )(go, w_out[layer], queries, window, low, high, mixed, lse)
        gkv = call(
            functools.partial(return_kernel, count, reach),
            shape((own, KV * TILE), f32),
            [
                pltpu.VMEM((reach, own, KV * TILE), bf16),
                pltpu.SemaphoreType.DMA((reach,)),
                pltpu.SemaphoreType.DMA((reach,)),
            ],
            collective_id=1,
            has_side_effects=True,
        )(gwin.reshape(reach + 1, own, KV * TILE))
        gqkv, upstream, gain_a = call(
            project_back_kernel,
            (
                shape((own, tiles), bf16),
                shape((own, width), f32),
                shape((1, width), f32),
            ),
        )(gq, gkv, cos_q, cos_kv, sin_all, w_in[layer], x_in, attn_gain[layer][None], gmid)
        gains.append((gain_a, gain_m))

        def halves(part):
            return lax.psum_scatter(part.astype(bf16), "tensor", scatter_dimension=0, tiled=True)

        ffn = [cols_by_cols(ggate, normed_m), cols_by_cols(gup, normed_m), cols_by_cols(hidden, gy)]
        own_gate, own_up, own_down = [
            lax.psum_scatter(halves(part), "dp", scatter_dimension=0, tiled=True) for part in ffn
        ]
        g_out = cols_by_cols(go, heads)
        g_in = cols_by_cols(gqkv, normed).reshape(H + KV, 2, HD, width)
        attn_part = jnp.concatenate(
            [
                g_in[:H, 0].reshape(H * HD, width),
                g_in[H:, 0].reshape(KV * HD, width),
                g_in[H:, 1].reshape(KV * HD, width),
                g_out,
            ],
            axis=0,
        ).astype(bf16)
        own_attn = lax.psum_scatter(attn_part, AXES, scatter_dimension=0, tiled=True)
        sums.append([value.astype(f32) for value in (own_attn, own_gate, own_up, own_down)])
    gains = gains[::-1]
    sums = sums[::-1]
    gain_sums = lax.psum(
        jnp.concatenate([row for pair in gains for row in pair], axis=0), AXES
    )
    attn_sum, gate_sum, up_sum, down_sum = [
        jnp.stack([entry[slot] for entry in sums], axis=0) for slot in range(4)
    ]
    return (
        stream,
        upstream,
        attn_sum,
        gain_sums[0::2],
        gate_sum,
        up_sum,
        down_sum,
        gain_sums[1::2],
    )


def solution(mesh):
    placed = (
        P(AXES, None),
        P(),
        P(),
        P(None, "tensor", None),
        P(None, "tensor", None),
        P(None, "tensor", None),
        P(),
        P(),
        P(AXES, None),
    )
    return jax.shard_map(
        body,
        mesh=mesh,
        in_specs=placed,
        out_specs=(
            P(AXES, None),
            P(AXES, None),
            P(None, AXES, None),
            P(),
            P(None, ("tensor", "dp"), None),
            P(None, ("tensor", "dp"), None),
            P(None, ("tensor", "dp"), None),
            P(),
        ),
        check_vma=False,
    )
```

```python
import functools

import jax
import jax.numpy as jnp
from jax import lax
from jax.experimental import pallas as pl
from jax.experimental.pallas import tpu as pltpu
from jax.sharding import PartitionSpec as P

H = 9
KV = 3
GROUPS = H // KV
HD = 64
TILE = 2 * HD
L_MAX = 2048

EPSILON = 1e-05
ROPE_BASE = 100000.0
MASKED = -1e30
MESH = pl.DeviceIdType.MESH
AXES = ("dp", "tensor")
VMEM_LIMIT = 56 * 1024 * 1024


def rows_by_rows(left, right):
    return lax.dot_general(
        left, right, (((1,), (1,)), ((), ())), preferred_element_type=jnp.float32
    )


def cols_by_cols(left, right):
    return lax.dot_general(
        left, right, (((0,), (0,)), ((), ())), preferred_element_type=jnp.float32
    )


def plain_dot(left, right):
    return jnp.dot(left, right, preferred_element_type=jnp.float32)


def sequence_start(places, starts):
    reached = starts[None, :] <= places[:, None]
    return jnp.max(jnp.where(reached, starts[None, :], -1), axis=1)


def rms_parts(values):
    inverse = lax.rsqrt(jnp.mean(values * values, axis=-1, keepdims=True) + EPSILON)
    return (values * inverse, inverse)


def norm_back(grad_out, ratio, inverse, gain_vec):
    scaled = grad_out * gain_vec
    input_grad = inverse * (scaled - ratio * jnp.mean(scaled * ratio, axis=-1, keepdims=True))
    return (input_grad, jnp.sum(grad_out * ratio, axis=0, keepdims=True))


def swap_halves(values):
    lane = lax.broadcasted_iota(jnp.int32, values.shape, 1)
    return jnp.where(
        lane < HD // 2,
        pltpu.roll(values, TILE - HD // 2, 1),
        pltpu.roll(values, HD // 2, 1),
    )


def call(kernel, out_shape, scratch=(), **params):
    return pl.pallas_call(
        kernel,
        out_shape=out_shape,
        scratch_shapes=list(scratch),
        compiler_params=pltpu.CompilerParams(vmem_limit_bytes=VMEM_LIMIT, **params),
    )


def project_kernel(x_ref, gain_ref, w_ref, cq_ref, ckv_ref, sn_ref, q_ref, kv_ref, a_ref):
    own = x_ref.shape[0]
    ratio, _ = rms_parts(x_ref[...])
    normed = (ratio * gain_ref[...]).astype(jnp.bfloat16)
    a_ref[...] = normed
    sines = sn_ref[...]
    for head in range(H + KV):
        lin = rows_by_rows(normed, w_ref[head * TILE : (head + 1) * TILE, :])
        cosines = cq_ref[...] if head < H else ckv_ref[...]
        turned = (lin * cosines + swap_halves(lin) * sines).astype(jnp.bfloat16)
        if head < H:
            rows = slice((head % GROUPS) * own, (head % GROUPS + 1) * own)
            q_ref[head // GROUPS, rows, :] = turned * jnp.bfloat16(0.125)
        else:
            kv_ref[:, (head - H) * TILE : (head - H + 1) * TILE] = turned


def mesh_id(index, pair):
    return {"dp": lax.div(index, pair), "tensor": lax.rem(index, pair)}


def greet(me, count, reach, step):
    barrier = pltpu.get_barrier_semaphore()
    pair = lax.axis_size("tensor")
    for by in range(1, reach + 1):
        sender = me + step * by

        @pl.when((sender >= 0) & (sender < count))
        def _():
            pl.semaphore_signal(
                barrier, inc=1, device_id=mesh_id(sender, pair), device_id_type=MESH
            )

    copied_to = jnp.minimum(count - 1 - me if step < 0 else me, reach)

    @pl.when(copied_to > 0)
    def _():
        pl.semaphore_wait(barrier, copied_to)


def fetch_kernel(count, reach, own_ref, window_ref, send_sem, recv_sem):
    pair = lax.axis_size("tensor")
    me = lax.axis_index("dp") * pair + lax.axis_index("tensor")
    greet(me, count, reach, -1)

    def send(by):
        return pltpu.make_async_remote_copy(
            src_ref=own_ref,
            dst_ref=window_ref.at[reach - by],
            send_sem=send_sem.at[by - 1],
            recv_sem=recv_sem.at[by - 1],
            device_id=mesh_id(me + by, pair),
            device_id_type=MESH,
        )

    for by in range(1, reach + 1):

        @pl.when(me + by < count)
        def _():
            send(by).start()

    window_ref[reach] = own_ref[...]
    for by in range(1, reach + 1):

        @pl.when(me - by < 0)
        def _():
            window_ref[reach - by] = jnp.zeros(own_ref.shape, own_ref.dtype)

    for by in range(1, reach + 1):

        @pl.when(me - by >= 0)
        def _():
            send(by).wait_recv()

        @pl.when(me + by < count)
        def _():
            send(by).wait_send()


def return_kernel(count, reach, grads_ref, sum_ref, held, send_sem, recv_sem):
    pair = lax.axis_size("tensor")
    me = lax.axis_index("dp") * pair + lax.axis_index("tensor")
    greet(me, count, reach, 1)

    def send(by):
        return pltpu.make_async_remote_copy(
            src_ref=grads_ref.at[reach - by],
            dst_ref=held.at[by - 1],
            send_sem=send_sem.at[by - 1],
            recv_sem=recv_sem.at[by - 1],
            device_id=mesh_id(me - by, pair),
            device_id_type=MESH,
        )

    for by in range(reach, 0, -1):

        @pl.when(me - by >= 0)
        def _():
            send(by).start()

    sum_ref[...] = grads_ref[reach].astype(jnp.float32)
    for by in range(1, reach + 1):

        @pl.when(me + by < count)
        def _():
            send(by).wait_recv()
            sum_ref[...] += held[by - 1].astype(jnp.float32)

        @pl.when(me - by >= 0)
        def _():
            send(by).wait_send()


def allowed_pairs(chunk, rows, low_ref, high_ref):
    place = chunk * rows + lax.broadcasted_iota(jnp.int32, (rows, low_ref.shape[1]), 0)
    return (place >= low_ref[...]) & (place <= high_ref[...])


def attend_kernel(
    chunk_rows,
    q_ref,
    win_ref,
    low_ref,
    high_ref,
    x_ref,
    wo_ref,
    gain_ref,
    wg_ref,
    wu_ref,
    wd_ref,
    x_out_ref,
    mid_ref,
    m_ref,
    gate_ref,
    up_ref,
    hidden_ref,
    o_ref,
    lse_ref,
    acc_ref,
    top_ref,
    total_ref,
):
    own = x_ref.shape[0]
    chunks = win_ref.shape[0] // chunk_rows
    acc_ref[...] = jnp.zeros_like(acc_ref)
    total_ref[...] = jnp.zeros_like(total_ref)
    top_ref[...] = jnp.full_like(top_ref, MASKED)

    def step(chunk, unused):
        allowed = allowed_pairs(chunk, chunk_rows, low_ref, high_ref)
        start = pl.multiple_of(chunk * chunk_rows, chunk_rows)
        for j in range(KV):
            tile = win_ref[pl.ds(start, chunk_rows), j * TILE : (j + 1) * TILE]
            scores = jnp.where(allowed, rows_by_rows(tile, q_ref[j]), MASKED)
            highest = top_ref[j]
            newest = jnp.maximum(highest, jnp.max(scores, axis=0, keepdims=True))
            terms = jnp.exp(scores - newest)
            decay = jnp.exp(highest - newest)
            top_ref[j] = newest
            total_ref[j] = total_ref[j] * decay + jnp.sum(terms, axis=0, keepdims=True)
            acc_ref[j] = acc_ref[j] * decay + cols_by_cols(tile, terms.astype(jnp.bfloat16))
        return unused

    lax.fori_loop(0, chunks, step, 0)
    middle = x_ref[...]
    for j in range(KV):
        lse_ref[j] = top_ref[j] + jnp.log(total_ref[j])
        mixed = (acc_ref[j] / total_ref[j]).T
        o_ref[j] = mixed
        low = mixed.astype(jnp.bfloat16)
        for g in range(GROUPS):
            middle = middle + plain_dot(low[g * own : (g + 1) * own], wo_ref[j * GROUPS + g])
    mid_ref[...] = middle
    ratio, _ = rms_parts(middle)
    normed = (ratio * gain_ref[...]).astype(jnp.bfloat16)
    m_ref[...] = normed
    gate = rows_by_rows(normed, wg_ref[...])
    up = rows_by_rows(normed, wu_ref[...])
    gate_ref[...] = gate
    up_ref[...] = up
    hidden = (gate * jax.nn.sigmoid(gate) * up).astype(jnp.bfloat16)
    hidden_ref[...] = hidden
    x_out_ref[...] = middle + plain_dot(hidden, wd_ref[...])


def mlp_back_kernel(
    gx_ref,
    mid_ref,
    gate_ref,
    up_ref,
    gain_ref,
    wg_ref,
    wu_ref,
    wd_ref,
    gy_ref,
    ggate_ref,
    gup_ref,
    gmid_ref,
    go_ref,
    ggain_ref,
):
    gx = gx_ref[...].astype(jnp.float32)
    gy = gx.astype(jnp.bfloat16)
    gy_ref[...] = gy
    gh = rows_by_rows(gy, wd_ref[...])
    gate = gate_ref[...]
    sig = jax.nn.sigmoid(gate)
    ggate = (gh * up_ref[...] * sig * (1.0 + gate * (1.0 - sig))).astype(jnp.bfloat16)
    gup = (gh * gate * sig).astype(jnp.bfloat16)
    ggate_ref[...] = ggate
    gup_ref[...] = gup
    gm = plain_dot(ggate, wg_ref[...]) + plain_dot(gup, wu_ref[...])
    ratio, inverse = rms_parts(mid_ref[...])
    back, ggain = norm_back(gm, ratio, inverse, gain_ref[...])
    ggain_ref[...] = ggain
    gmid = gx + back
    gmid_ref[...] = gmid
    go_ref[...] = gmid.astype(jnp.bfloat16)


def attend_back_kernel(
    chunk_rows,
    go_ref,
    wo_ref,
    q_ref,
    win_ref,
    low_ref,
    high_ref,
    o_ref,
    lse_ref,
    gq_ref,
    gwin_ref,
    grad_ref,
    delta_ref,
    acc_ref,
):
    own = go_ref.shape[0]
    chunks = win_ref.shape[0] // chunk_rows
    go = go_ref[...]
    lane = lax.broadcasted_iota(jnp.int32, (GROUPS * own, TILE), 1)
    for j in range(KV):
        for g in range(GROUPS):
            grad_ref[j, g * own : (g + 1) * own, :] = rows_by_rows(
                go, wo_ref[j * GROUPS + g]
            ).astype(jnp.bfloat16)
        product = jnp.where(lane >= HD, grad_ref[j].astype(jnp.float32) * o_ref[j], 0.0)
        delta_ref[j] = jnp.sum(product.T, axis=0, keepdims=True)
    acc_ref[...] = jnp.zeros_like(acc_ref)

    def step(chunk, unused):
        allowed = allowed_pairs(chunk, chunk_rows, low_ref, high_ref)
        start = pl.multiple_of(chunk * chunk_rows, chunk_rows)
        for j in range(KV):
            tile = win_ref[pl.ds(start, chunk_rows), j * TILE : (j + 1) * TILE]
            queries = q_ref[j]
            grads = grad_ref[j]
            scores = rows_by_rows(tile, queries) - lse_ref[j]
            weights = jnp.exp(jnp.where(allowed, scores, MASKED))
            slopes = rows_by_rows(tile, grads) - delta_ref[j]
            score_grads = (weights * slopes).astype(jnp.bfloat16)
            acc_ref[j] += cols_by_cols(tile, score_grads)
            both = plain_dot(score_grads, queries) + plain_dot(
                weights.astype(jnp.bfloat16), grads
            )
            gwin_ref[pl.ds(start, chunk_rows), j * TILE : (j + 1) * TILE] = both.astype(
                jnp.bfloat16
            )
        return unused

    lax.fori_loop(0, chunks, step, 0)
    for j in range(KV):
        gq_ref[j] = (0.125 * acc_ref[j]).T


def project_back_kernel(
    gq_ref, gkv_ref, cq_ref, ckv_ref, sn_ref, w_ref, x_ref, gain_ref, gmid_ref, gqkv_ref, gx_ref, ggain_ref
):
    own = x_ref.shape[0]
    sines = -sn_ref[...]
    for head in range(H + KV):
        if head < H:
            rows = slice((head % GROUPS) * own, (head % GROUPS + 1) * own)
            lin = gq_ref[head // GROUPS, rows, :]
            cosines = cq_ref[...]
        else:
            lin = gkv_ref[:, (head - H) * TILE : (head - H + 1) * TILE]
            cosines = ckv_ref[...]
        turned = (lin * cosines + swap_halves(lin) * sines).astype(jnp.bfloat16)
        gqkv_ref[:, head * TILE : (head + 1) * TILE] = turned
    grad_normed = plain_dot(gqkv_ref[...], w_ref[...])
    ratio, inverse = rms_parts(x_ref[...])
    back, ggain = norm_back(grad_normed, ratio, inverse, gain_ref[...])
    ggain_ref[...] = ggain
    gx_ref[...] = gmid_ref[...] + back


def sum_kernel(sizes, orders, *refs):
    parts = len(orders)
    pair, across, up, deep = sizes
    core = lax.axis_index("tensor")
    index = lax.axis_index("dp")
    place = {
        "t": core,
        "x": lax.rem(index, across),
        "y": lax.rem(lax.div(index, across), up),
        "z": lax.div(index, across * up),
    }
    extent = {"t": pair, "x": across, "y": up, "z": deep}
    stages = len(orders[0])
    steps = max(extent.values())
    ins, gain_ref = refs[:parts], refs[parts]
    outs, gain_out = refs[parts + 1 : 2 * parts + 1], refs[2 * parts + 1]
    rest = list(refs[2 * parts + 2 :])
    kept = [[rest.pop(0) for _ in range(stages - 1)] for _ in range(parts)]
    held = [[rest.pop(0) for _ in range(stages)] for _ in range(parts)]
    gain_held = [rest.pop(0) for _ in range(stages)]
    gain_sum = rest.pop(0)
    send_sem, recv_sem, gain_send, gain_recv = rest

    def partner(axis, coordinate):
        at = dict(place)
        at[axis] = coordinate
        return {"dp": (at["z"] * up + at["y"]) * across + at["x"], "tensor": at["t"]}

    barrier = pltpu.get_barrier_semaphore()
    partners = 0
    for axis, size in extent.items():
        for by in range(1, size):
            partners += 1
            pl.semaphore_signal(
                barrier,
                inc=1,
                device_id=partner(axis, lax.rem(place[axis] + by, size)),
                device_id_type=MESH,
            )
    pl.semaphore_wait(barrier, partners)

    def copies(part, stage):
        axis = orders[part][stage]
        size = extent[axis]
        source = ins[part] if stage == 0 else kept[part][stage - 1]
        blocks = source.shape[0] // size
        made = []
        for by in range(1, size):
            target = lax.rem(place[axis] + by, size)
            made.append(
                pltpu.make_async_remote_copy(
                    src_ref=source.at[pl.ds(target * blocks, blocks)],
                    dst_ref=held[part][stage].at[pl.ds((by - 1) * blocks, blocks)],
                    send_sem=send_sem.at[(part * stages + stage) * steps + by],
                    recv_sem=recv_sem.at[(part * stages + stage) * steps + by],
                    device_id=partner(axis, target),
                    device_id_type=MESH,
                )
            )
        return made

    def gain_copies(stage):
        axis = orders[0][stage]
        size = extent[axis]
        return [
            pltpu.make_async_remote_copy(
                src_ref=gain_ref if stage == 0 else gain_sum.at[stage - 1],
                dst_ref=gain_held[stage].at[place[axis]],
                send_sem=gain_send.at[stage * steps + by],
                recv_sem=gain_recv.at[stage * steps + by],
                device_id=partner(axis, lax.rem(place[axis] + by, size)),
                device_id_type=MESH,
            )
            for by in range(1, size)
        ]

    def start(part, stage):
        for copy in copies(part, stage):
            copy.start()

    def finish(part, stage):
        for copy in copies(part, stage):
            copy.wait_recv()
        axis = orders[part][stage]
        size = extent[axis]
        source = ins[part] if stage == 0 else kept[part][stage - 1]
        blocks = source.shape[0] // size

        def add(block, unused):
            value = source[place[axis] * blocks + block].astype(jnp.float32)
            for by in range(1, size):
                value += held[part][stage][(by - 1) * blocks + block].astype(jnp.float32)
            if stage < stages - 1:
                kept[part][stage][block] = value.astype(jnp.bfloat16)
            else:
                outs[part][...] = value
            return unused

        lax.fori_loop(0, blocks, add, 0)

    def start_gain(stage):
        for copy in gain_copies(stage):
            copy.start()

    def finish_gain(stage):
        axis = orders[0][stage]
        for by, copy in enumerate(gain_copies(stage)):
            copy.wait_recv()
        gain_held[stage][place[axis]] = gain_ref[...] if stage == 0 else gain_sum[stage - 1]
        value = gain_held[stage][0]
        for other in range(1, extent[axis]):
            value += gain_held[stage][other]
        gain_sum[stage] = value

    for part in range(parts):
        start(part, 0)
    start_gain(0)
    for stage in range(stages):
        for part in range(parts):
            finish(part, stage)
            if stage < stages - 1:
                start(part, stage + 1)
        finish_gain(stage)
        if stage < stages - 1:
            start_gain(stage + 1)
    gain_out[...] = gain_sum[stages - 1]
    for stage in range(stages):
        for part in range(parts):
            for copy in copies(part, stage):
                copy.wait_send()
        for copy in gain_copies(stage):
            copy.wait_send()


def directions(count):
    side = round((count // 2) ** (1 / 3))
    if side > 0 and 2 * side * side * side == count:
        return side, side, 2 * side
    return 1, 1, count


def sum_grads(layer_parts, gains):
    bf16 = jnp.bfloat16
    pair = lax.axis_size("tensor")
    across, up, deep = directions(lax.axis_size("dp"))
    extent = {"t": pair, "x": across, "y": up, "z": deep}
    width = gains.shape[1]
    orders = ["txyz" if part % 2 == 0 else "tyxz" for part in range(len(layer_parts))]
    chips = across * up * deep
    stacked = []
    for order, (attn, *ffn) in zip(orders, layer_parts):
        pieces = attn.shape[0] // (chips * pair)
        split = [jnp.transpose(attn.reshape(chips, pair, pieces, width), (1, 0, 2, 3))]
        split += [part.reshape(pair, chips, pieces, width) for part in ffn]
        whole = jnp.stack(split, axis=2).reshape(
            pair, deep, up, across, len(split) * pieces, width
        )
        turn = (0, 3, 2, 1, 4, 5) if order == "txyz" else (0, 2, 3, 1, 4, 5)
        stacked.append(
            jnp.transpose(whole, turn).reshape(pair * chips, len(split) * pieces, width)
        )
    rows = stacked[0].shape[1]
    stages = 4
    kept, held = [], []
    for order in orders:
        blocks = pair * chips
        for stage, axis in enumerate(order):
            blocks //= extent[axis]
            if stage < stages - 1:
                kept.append(pltpu.VMEM((blocks, rows, width), bf16))
            held.append(
                pltpu.VMEM((max(extent[axis] - 1, 1) * blocks, rows, width), bf16)
            )
    gain_held = [pltpu.VMEM((extent[axis],) + gains.shape, jnp.float32) for axis in orders[0]]
    steps = max(extent.values())
    slots = len(orders) * stages * steps
    *sums, gain_sums = call(
        functools.partial(sum_kernel, (pair, across, up, deep), tuple(orders)),
        tuple(jax.ShapeDtypeStruct((rows, width), jnp.float32) for _ in orders)
        + (jax.ShapeDtypeStruct(gains.shape, jnp.float32),),
        kept
        + held
        + gain_held
        + [
            pltpu.VMEM((stages,) + gains.shape, jnp.float32),
            pltpu.SemaphoreType.DMA((slots,)),
            pltpu.SemaphoreType.DMA((slots,)),
            pltpu.SemaphoreType.DMA((stages * steps,)),
            pltpu.SemaphoreType.DMA((stages * steps,)),
        ],
        collective_id=2,
        has_side_effects=True,
    )(*stacked, gains)
    return [jnp.split(value, 4, axis=0) for value in sums], gain_sums


def body(tokens, w_attn, attn_gain, w_gate, w_up, w_down, mlp_gain, seq_lengths, cotangent):
    own, width = tokens.shape
    layers = w_attn.shape[0]
    count = lax.axis_size("dp") * lax.axis_size("tensor")
    qkv_rows = (H + 2 * KV) * HD
    reach = min((L_MAX + own - 2) // own, count - 1)
    window_rows = (reach + 1) * own
    chunk_rows = 2 * own if (reach + 1) % 2 == 0 else own
    tiles = (H + KV) * TILE
    f32, bf16 = jnp.float32, jnp.bfloat16
    shape = jax.ShapeDtypeStruct

    seq_ends = jnp.cumsum(seq_lengths)
    starts = seq_ends - seq_lengths
    first_place = lax.axis_index(AXES) * own
    places = first_place + jnp.arange(own, dtype=jnp.int32)
    begin = sequence_start(places, starts)
    first_key = first_place - reach * own
    low = jnp.tile(begin - first_key, GROUPS)[None, :]
    high = jnp.tile(places - first_key, GROUPS)[None, :]
    frequencies = jnp.power(ROPE_BASE, -2.0 * jnp.arange(HD // 2, dtype=f32) / HD)
    angles = (places - begin).astype(f32)[:, None] * frequencies[None, :]
    cosines, sines = jnp.cos(angles), jnp.sin(angles)
    zeros, ones = jnp.zeros((own, HD), f32), jnp.ones((own, HD), f32)
    cos_q = jnp.concatenate([cosines, cosines, zeros], axis=1)
    cos_kv = jnp.concatenate([cosines, cosines, ones], axis=1)
    sin_all = jnp.concatenate([-sines, sines, zeros], axis=1)

    gate_all = lax.all_gather(w_gate, "tensor", axis=1, tiled=True)
    up_all = lax.all_gather(w_up, "tensor", axis=1, tiled=True)
    down_all = lax.all_gather(w_down, "tensor", axis=1, tiled=True)
    q_rows = w_attn[:, : H * HD].reshape(layers, H, HD, width)
    k_rows = w_attn[:, H * HD : (H + KV) * HD].reshape(layers, KV, HD, width)
    v_rows = w_attn[:, (H + KV) * HD : qkv_rows].reshape(layers, KV, HD, width)
    w_in = jnp.concatenate(
        [
            jnp.pad(q_rows, ((0, 0), (0, 0), (0, HD), (0, 0))),
            jnp.concatenate([k_rows, v_rows], axis=2),
        ],
        axis=1,
    ).reshape(layers, tiles, width)
    w_out = jnp.pad(
        jnp.swapaxes(w_attn[:, qkv_rows:], 1, 2).reshape(layers, H, HD, width),
        ((0, 0), (0, 0), (HD, 0), (0, 0)),
    )

    stream = tokens.astype(f32)
    stored = []
    for layer in range(layers):
        queries, kv_own, normed = call(
            project_kernel,
            (
                shape((KV, GROUPS * own, TILE), bf16),
                shape((own, KV * TILE), bf16),
                shape((own, width), bf16),
            ),
        )(stream, attn_gain[layer][None], w_in[layer], cos_q, cos_kv, sin_all)
        window = call(
            functools.partial(fetch_kernel, count, reach),
            shape((reach + 1, own, KV * TILE), bf16),
            [pltpu.SemaphoreType.DMA((reach,)), pltpu.SemaphoreType.DMA((reach,))],
            collective_id=0,
            has_side_effects=True,
        )(kv_own).reshape(window_rows, KV * TILE)
        hidden_rows = gate_all.shape[1]
        x_out, middle, normed_m, gate, up, hidden, mixed, lse = call(
            functools.partial(attend_kernel, chunk_rows),
            (
                shape((own, width), f32),
                shape((own, width), f32),
                shape((own, width), bf16),
                shape((own, hidden_rows), f32),
                shape((own, hidden_rows), f32),
                shape((own, hidden_rows), bf16),
                shape((KV, GROUPS * own, TILE), f32),
                shape((KV, 1, GROUPS * own), f32),
            ),
            [
                pltpu.VMEM((KV, TILE, GROUPS * own), f32),
                pltpu.VMEM((KV, 1, GROUPS * own), f32),
                pltpu.VMEM((KV, 1, GROUPS * own), f32),
            ],
        )(
            queries,
            window,
            low,
            high,
            stream,
            w_out[layer],
            mlp_gain[layer][None],
            gate_all[layer],
            up_all[layer],
            down_all[layer],
        )
        stored.append((stream, queries, normed, window, middle, normed_m, gate, up, hidden, mixed, lse))
        stream = x_out

    upstream = cotangent
    gains = []
    parts = []
    for layer in reversed(range(layers)):
        x_in, queries, normed, window, middle, normed_m, gate, up, hidden, mixed, lse = stored[layer]
        hidden_rows = gate_all.shape[1]
        gy, ggate, gup, gmid, go, gain_m = call(
            mlp_back_kernel,
            (
                shape((own, width), bf16),
                shape((own, hidden_rows), bf16),
                shape((own, hidden_rows), bf16),
                shape((own, width), f32),
                shape((own, width), bf16),
                shape((1, width), f32),
            ),
        )(
            upstream,
            middle,
            gate,
            up,
            mlp_gain[layer][None],
            gate_all[layer],
            up_all[layer],
            down_all[layer],
        )
        heads = jnp.transpose(
            mixed.reshape(H, own, TILE)[:, :, HD:].astype(bf16), (1, 0, 2)
        ).reshape(own, H * HD)
        gq, gwin = call(
            functools.partial(attend_back_kernel, chunk_rows),
            (
                shape((KV, GROUPS * own, TILE), f32),
                shape((window_rows, KV * TILE), bf16),
            ),
            [
                pltpu.VMEM((KV, GROUPS * own, TILE), bf16),
                pltpu.VMEM((KV, 1, GROUPS * own), f32),
                pltpu.VMEM((KV, TILE, GROUPS * own), f32),
            ],
        )(go, w_out[layer], queries, window, low, high, mixed, lse)
        gkv = call(
            functools.partial(return_kernel, count, reach),
            shape((own, KV * TILE), f32),
            [
                pltpu.VMEM((reach, own, KV * TILE), bf16),
                pltpu.SemaphoreType.DMA((reach,)),
                pltpu.SemaphoreType.DMA((reach,)),
            ],
            collective_id=1,
            has_side_effects=True,
        )(gwin.reshape(reach + 1, own, KV * TILE))
        gqkv, upstream, gain_a = call(
            project_back_kernel,
            (
                shape((own, tiles), bf16),
                shape((own, width), f32),
                shape((1, width), f32),
            ),
        )(gq, gkv, cos_q, cos_kv, sin_all, w_in[layer], x_in, attn_gain[layer][None], gmid)
        gains.append((gain_a, gain_m))

        ffn = [
            cols_by_cols(left, right).astype(bf16)
            for left, right in ((ggate, normed_m), (gup, normed_m), (hidden, gy))
        ]
        g_out = cols_by_cols(go, heads)
        g_in = cols_by_cols(gqkv, normed).reshape(H + KV, 2, HD, width)
        attn_part = jnp.concatenate(
            [
                g_in[:H, 0].reshape(H * HD, width),
                g_in[H:, 0].reshape(KV * HD, width),
                g_in[H:, 1].reshape(KV * HD, width),
                g_out,
            ],
            axis=0,
        ).astype(bf16)
        parts.append([attn_part, *ffn])
    rows = [row for pair in gains[::-1] for row in pair]
    rows.append(jnp.zeros((-len(rows) % 8, width), f32))
    sums, gain_sums = sum_grads(parts[::-1], jnp.concatenate(rows, axis=0))
    attn_sum, gate_sum, up_sum, down_sum = [
        jnp.stack([entry[slot] for entry in sums], axis=0) for slot in range(4)
    ]
    gain_sums = gain_sums[: 2 * layers]
    return (
        stream,
        upstream,
        attn_sum,
        gain_sums[0::2],
        gate_sum,
        up_sum,
        down_sum,
        gain_sums[1::2],
    )


def solution(mesh):
    placed = (
        P(AXES, None),
        P(),
        P(),
        P(None, "tensor", None),
        P(None, "tensor", None),
        P(None, "tensor", None),
        P(),
        P(),
        P(AXES, None),
    )
    return jax.shard_map(
        body,
        mesh=mesh,
        in_specs=placed,
        out_specs=(
            P(AXES, None),
            P(AXES, None),
            P(None, AXES, None),
            P(),
            P(None, ("tensor", "dp"), None),
            P(None, ("tensor", "dp"), None),
            P(None, ("tensor", "dp"), None),
            P(),
        ),
        check_vma=False,
    )
```

```python
import functools

import jax
import jax.numpy as jnp
from jax import lax
from jax.experimental import pallas as pl
from jax.experimental.pallas import tpu as pltpu
from jax.sharding import PartitionSpec as P

H = 9
KV = 3
GROUPS = H // KV
HD = 64
TILE = 2 * HD
L_MAX = 2048

EPSILON = 1e-05
ROPE_BASE = 100000.0
MASKED = -1e30
MESH = pl.DeviceIdType.MESH
AXES = ("dp", "tensor")
VMEM_LIMIT = 56 * 1024 * 1024


def rows_by_rows(left, right):
    return lax.dot_general(
        left, right, (((1,), (1,)), ((), ())), preferred_element_type=jnp.float32
    )


def cols_by_cols(left, right):
    return lax.dot_general(
        left, right, (((0,), (0,)), ((), ())), preferred_element_type=jnp.float32
    )


def plain_dot(left, right):
    return jnp.dot(left, right, preferred_element_type=jnp.float32)


def sequence_start(places, starts):
    reached = starts[None, :] <= places[:, None]
    return jnp.max(jnp.where(reached, starts[None, :], -1), axis=1)


def rms_parts(values):
    inverse = lax.rsqrt(jnp.mean(values * values, axis=-1, keepdims=True) + EPSILON)
    return (values * inverse, inverse)


def norm_back(grad_out, ratio, inverse, gain_vec):
    scaled = grad_out * gain_vec
    input_grad = inverse * (scaled - ratio * jnp.mean(scaled * ratio, axis=-1, keepdims=True))
    return (input_grad, jnp.sum(grad_out * ratio, axis=0, keepdims=True))


def swap_halves(values):
    lane = lax.broadcasted_iota(jnp.int32, values.shape, 1)
    return jnp.where(
        lane < HD // 2,
        pltpu.roll(values, TILE - HD // 2, 1),
        pltpu.roll(values, HD // 2, 1),
    )


def call(kernel, out_shape, scratch=(), **params):
    return pl.pallas_call(
        kernel,
        out_shape=out_shape,
        scratch_shapes=list(scratch),
        compiler_params=pltpu.CompilerParams(vmem_limit_bytes=VMEM_LIMIT, **params),
    )


def project_kernel(x_ref, gain_ref, w_ref, cq_ref, ckv_ref, sn_ref, q_ref, kv_ref, a_ref):
    own = x_ref.shape[0]
    ratio, _ = rms_parts(x_ref[...])
    normed = (ratio * gain_ref[...]).astype(jnp.bfloat16)
    a_ref[...] = normed
    sines = sn_ref[...]
    for head in range(H + KV):
        lin = rows_by_rows(normed, w_ref[head * TILE : (head + 1) * TILE, :])
        cosines = cq_ref[...] if head < H else ckv_ref[...]
        turned = (lin * cosines + swap_halves(lin) * sines).astype(jnp.bfloat16)
        if head < H:
            rows = slice((head % GROUPS) * own, (head % GROUPS + 1) * own)
            q_ref[head // GROUPS, rows, :] = turned * jnp.bfloat16(0.125)
        else:
            kv_ref[:, (head - H) * TILE : (head - H + 1) * TILE] = turned


def mesh_id(index, pair):
    return {"dp": lax.div(index, pair), "tensor": lax.rem(index, pair)}


def greet(me, count, reach, step, senders_pair, copies_pair):
    barrier = pltpu.get_barrier_semaphore()
    core = lax.rem(me, 2)
    far_sender = 0 if step < 0 else 1
    waits = jnp.where(copies_pair, 1, 0)
    for by in list(range(2, reach, 2)) + [reach]:
        sender, target = me + step * by, me - step * by
        hears = (sender >= 0) & (sender < count)
        sends = (target >= 0) & (target < count)
        if by == reach:
            hears = hears & (core == far_sender)
            sends = sends & (core == 1 - far_sender)

        @pl.when(hears)
        def _():
            pl.semaphore_signal(
                barrier, inc=1, device_id=mesh_id(sender, 2), device_id_type=MESH
            )

        waits = waits + jnp.where(sends, 1, 0)

    @pl.when(senders_pair)
    def _():
        pl.semaphore_signal(
            barrier, inc=1, device_id=mesh_id(me + 1 - 2 * core, 2), device_id_type=MESH
        )

    @pl.when(waits > 0)
    def _():
        pl.semaphore_wait(barrier, waits)


def fetch_kernel(count, reach, own_ref, window_ref, send_sem, recv_sem, pass_sem):
    core = lax.axis_index("tensor")
    me = lax.axis_index("dp") * 2 + core
    sibling = me + 1 - 2 * core
    greet(me, count, reach, -1, (core == 1) | (me > 0), (core == 0) | (me > 1))

    def send(by):
        return pltpu.make_async_remote_copy(
            src_ref=own_ref,
            dst_ref=window_ref.at[reach - by],
            send_sem=send_sem.at[by],
            recv_sem=recv_sem.at[by],
            device_id=mesh_id(me + by, 2),
            device_id_type=MESH,
        )

    def hand_over(by):
        there = by + 1 - 2 * core
        return pltpu.make_async_remote_copy(
            src_ref=own_ref if by == 0 else window_ref.at[reach - by],
            dst_ref=window_ref.at[reach - there],
            send_sem=pass_sem.at[by],
            recv_sem=recv_sem.at[there],
            device_id=mesh_id(sibling, 2),
            device_id_type=MESH,
        )

    even = list(range(2, reach, 2))
    for by in even:

        @pl.when(me + by < count)
        def _():
            send(by).start()

    @pl.when((core == 1) & (me + reach < count))
    def _():
        send(reach).start()

    @pl.when(core == 0)
    def _():
        hand_over(0).start()

    window_ref[reach] = own_ref[...]
    for by in range(1, reach + 1):

        @pl.when(me - by < 0)
        def _():
            window_ref[reach - by] = jnp.zeros(own_ref.shape, own_ref.dtype)

    for by in even:

        @pl.when(me - by >= 0)
        def _():
            send(by).wait_recv()
            hand_over(by).start()

    for by in range(1, reach + 1, 2):

        @pl.when(me - by >= 0)
        def _():
            send(by).wait_recv()

    for by in even:

        @pl.when(me - by >= 0)
        def _():
            hand_over(by).wait_send()

        @pl.when(me + by < count)
        def _():
            send(by).wait_send()

    @pl.when((core == 1) & (me + reach < count))
    def _():
        send(reach).wait_send()

    @pl.when(core == 0)
    def _():
        hand_over(0).wait_send()


def return_kernel(
    count, reach, grads_ref, sum_ref, near, joined, held, send_sem, recv_sem, pass_sem, near_sem
):
    core = lax.axis_index("tensor")
    me = lax.axis_index("dp") * 2 + core
    sibling = me + 1 - 2 * core
    greet(me, count, reach, 1, (core == 0) | (me > 1), (core == 1) | (me > 0))
    even = list(range(2, reach, 2))

    def hand_over(by):
        slot = (by + 1) // 2 - core
        return pltpu.make_async_remote_copy(
            src_ref=grads_ref.at[reach - by],
            dst_ref=near.at[slot],
            send_sem=pass_sem.at[by],
            recv_sem=near_sem.at[slot],
            device_id=mesh_id(sibling, 2),
            device_id_type=MESH,
        )

    def taken(slot):
        return pltpu.make_async_remote_copy(
            src_ref=grads_ref.at[0],
            dst_ref=near.at[slot],
            send_sem=pass_sem.at[0],
            recv_sem=near_sem.at[slot],
            device_id=mesh_id(sibling, 2),
            device_id_type=MESH,
        )

    def send(by):
        return pltpu.make_async_remote_copy(
            src_ref=grads_ref.at[0] if by == reach else joined.at[by // 2 - 1],
            dst_ref=held.at[by // 2 - 1 + by % 2],
            send_sem=send_sem.at[by],
            recv_sem=recv_sem.at[by],
            device_id=mesh_id(me - by, 2),
            device_id_type=MESH,
        )

    @pl.when((core == 0) & (me - reach >= 0))
    def _():
        send(reach).start()

    for by in range(reach, 0, -2):
        wanted = me - by >= 0
        if by == reach:
            wanted = wanted & (core == 1)

        @pl.when(wanted)
        def _():
            hand_over(by).start()

    for by in even[::-1]:

        @pl.when(me - by >= 0)
        def _():
            taken(by // 2).wait_recv()
            joined[by // 2 - 1] = (
                grads_ref[reach - by].astype(jnp.float32) + near[by // 2].astype(jnp.float32)
            ).astype(jnp.bfloat16)
            send(by).start()

    sum_ref[...] = grads_ref[reach].astype(jnp.float32)

    @pl.when(core == 0)
    def _():
        taken(0).wait_recv()
        sum_ref[...] += near[0].astype(jnp.float32)

    for by in even + [reach]:
        comes = me + by < count
        if by == reach:
            comes = comes & (core == 1)

        @pl.when(comes)
        def _():
            send(by).wait_recv()
            sum_ref[...] += held[by // 2 - 1 + by % 2].astype(jnp.float32)

    for by in even:

        @pl.when(me - by >= 0)
        def _():
            send(by).wait_send()

    @pl.when((core == 0) & (me - reach >= 0))
    def _():
        send(reach).wait_send()

    for by in range(reach, 0, -2):
        wanted = me - by >= 0
        if by == reach:
            wanted = wanted & (core == 1)

        @pl.when(wanted)
        def _():
            hand_over(by).wait_send()


def allowed_pairs(chunk, rows, low_ref, high_ref):
    place = chunk * rows + lax.broadcasted_iota(jnp.int32, (rows, low_ref.shape[1]), 0)
    return (place >= low_ref[...]) & (place <= high_ref[...])


def attend_kernel(
    chunk_rows,
    q_ref,
    win_ref,
    low_ref,
    high_ref,
    x_ref,
    wo_ref,
    gain_ref,
    wg_ref,
    wu_ref,
    wd_ref,
    x_out_ref,
    mid_ref,
    m_ref,
    gate_ref,
    up_ref,
    hidden_ref,
    o_ref,
    lse_ref,
    acc_ref,
    top_ref,
    total_ref,
):
    own = x_ref.shape[0]
    chunks = win_ref.shape[0] // chunk_rows
    acc_ref[...] = jnp.zeros_like(acc_ref)
    total_ref[...] = jnp.zeros_like(total_ref)
    top_ref[...] = jnp.full_like(top_ref, MASKED)

    def step(chunk, unused):
        allowed = allowed_pairs(chunk, chunk_rows, low_ref, high_ref)
        start = pl.multiple_of(chunk * chunk_rows, chunk_rows)
        for j in range(KV):
            tile = win_ref[pl.ds(start, chunk_rows), j * TILE : (j + 1) * TILE]
            scores = jnp.where(allowed, rows_by_rows(tile, q_ref[j]), MASKED)
            highest = top_ref[j]
            newest = jnp.maximum(highest, jnp.max(scores, axis=0, keepdims=True))
            terms = jnp.exp(scores - newest)
            decay = jnp.exp(highest - newest)
            top_ref[j] = newest
            total_ref[j] = total_ref[j] * decay + jnp.sum(terms, axis=0, keepdims=True)
            acc_ref[j] = acc_ref[j] * decay + cols_by_cols(tile, terms.astype(jnp.bfloat16))
        return unused

    lax.fori_loop(0, chunks, step, 0)
    middle = x_ref[...]
    for j in range(KV):
        lse_ref[j] = top_ref[j] + jnp.log(total_ref[j])
        mixed = (acc_ref[j] / total_ref[j]).T
        o_ref[j] = mixed
        low = mixed.astype(jnp.bfloat16)
        for g in range(GROUPS):
            middle = middle + plain_dot(low[g * own : (g + 1) * own], wo_ref[j * GROUPS + g])
    mid_ref[...] = middle
    ratio, _ = rms_parts(middle)
    normed = (ratio * gain_ref[...]).astype(jnp.bfloat16)
    m_ref[...] = normed
    gate = rows_by_rows(normed, wg_ref[...])
    up = rows_by_rows(normed, wu_ref[...])
    gate_ref[...] = gate
    up_ref[...] = up
    hidden = (gate * jax.nn.sigmoid(gate) * up).astype(jnp.bfloat16)
    hidden_ref[...] = hidden
    x_out_ref[...] = middle + plain_dot(hidden, wd_ref[...])


def mlp_back_kernel(
    gx_ref,
    mid_ref,
    gate_ref,
    up_ref,
    gain_ref,
    wg_ref,
    wu_ref,
    wd_ref,
    gy_ref,
    ggate_ref,
    gup_ref,
    gmid_ref,
    go_ref,
    ggain_ref,
):
    gx = gx_ref[...].astype(jnp.float32)
    gy = gx.astype(jnp.bfloat16)
    gy_ref[...] = gy
    gh = rows_by_rows(gy, wd_ref[...])
    gate = gate_ref[...]
    sig = jax.nn.sigmoid(gate)
    ggate = (gh * up_ref[...] * sig * (1.0 + gate * (1.0 - sig))).astype(jnp.bfloat16)
    gup = (gh * gate * sig).astype(jnp.bfloat16)
    ggate_ref[...] = ggate
    gup_ref[...] = gup
    gm = plain_dot(ggate, wg_ref[...]) + plain_dot(gup, wu_ref[...])
    ratio, inverse = rms_parts(mid_ref[...])
    back, ggain = norm_back(gm, ratio, inverse, gain_ref[...])
    ggain_ref[...] = ggain
    gmid = gx + back
    gmid_ref[...] = gmid
    go_ref[...] = gmid.astype(jnp.bfloat16)


def attend_back_kernel(
    chunk_rows,
    go_ref,
    wo_ref,
    q_ref,
    win_ref,
    low_ref,
    high_ref,
    o_ref,
    lse_ref,
    gq_ref,
    gwin_ref,
    grad_ref,
    delta_ref,
    acc_ref,
):
    own = go_ref.shape[0]
    chunks = win_ref.shape[0] // chunk_rows
    go = go_ref[...]
    lane = lax.broadcasted_iota(jnp.int32, (GROUPS * own, TILE), 1)
    for j in range(KV):
        for g in range(GROUPS):
            grad_ref[j, g * own : (g + 1) * own, :] = rows_by_rows(
                go, wo_ref[j * GROUPS + g]
            ).astype(jnp.bfloat16)
        product = jnp.where(lane >= HD, grad_ref[j].astype(jnp.float32) * o_ref[j], 0.0)
        delta_ref[j] = jnp.sum(product.T, axis=0, keepdims=True)
    acc_ref[...] = jnp.zeros_like(acc_ref)

    def step(chunk, unused):
        allowed = allowed_pairs(chunk, chunk_rows, low_ref, high_ref)
        start = pl.multiple_of(chunk * chunk_rows, chunk_rows)
        for j in range(KV):
            tile = win_ref[pl.ds(start, chunk_rows), j * TILE : (j + 1) * TILE]
            queries = q_ref[j]
            grads = grad_ref[j]
            scores = rows_by_rows(tile, queries) - lse_ref[j]
            weights = jnp.exp(jnp.where(allowed, scores, MASKED))
            slopes = rows_by_rows(tile, grads) - delta_ref[j]
            score_grads = (weights * slopes).astype(jnp.bfloat16)
            acc_ref[j] += cols_by_cols(tile, score_grads)
            both = plain_dot(score_grads, queries) + plain_dot(
                weights.astype(jnp.bfloat16), grads
            )
            gwin_ref[pl.ds(start, chunk_rows), j * TILE : (j + 1) * TILE] = both.astype(
                jnp.bfloat16
            )
        return unused

    lax.fori_loop(0, chunks, step, 0)
    for j in range(KV):
        gq_ref[j] = (0.125 * acc_ref[j]).T


def project_back_kernel(
    gq_ref, gkv_ref, cq_ref, ckv_ref, sn_ref, w_ref, x_ref, gain_ref, gmid_ref, gqkv_ref, gx_ref, ggain_ref
):
    own = x_ref.shape[0]
    sines = -sn_ref[...]
    for head in range(H + KV):
        if head < H:
            rows = slice((head % GROUPS) * own, (head % GROUPS + 1) * own)
            lin = gq_ref[head // GROUPS, rows, :]
            cosines = cq_ref[...]
        else:
            lin = gkv_ref[:, (head - H) * TILE : (head - H + 1) * TILE]
            cosines = ckv_ref[...]
        turned = (lin * cosines + swap_halves(lin) * sines).astype(jnp.bfloat16)
        gqkv_ref[:, head * TILE : (head + 1) * TILE] = turned
    grad_normed = plain_dot(gqkv_ref[...], w_ref[...])
    ratio, inverse = rms_parts(x_ref[...])
    back, ggain = norm_back(grad_normed, ratio, inverse, gain_ref[...])
    ggain_ref[...] = ggain
    gx_ref[...] = gmid_ref[...] + back


def sum_kernel(sizes, orders, *refs):
    parts = len(orders)
    pair, across, up, deep = sizes
    core = lax.axis_index("tensor")
    index = lax.axis_index("dp")
    place = {
        "t": core,
        "x": lax.rem(index, across),
        "y": lax.rem(lax.div(index, across), up),
        "z": lax.div(index, across * up),
    }
    extent = {"t": pair, "x": across, "y": up, "z": deep}
    stages = len(orders[0])
    steps = max(extent.values())
    ins, gain_ref = refs[:parts], refs[parts]
    outs, gain_out = refs[parts + 1 : 2 * parts + 1], refs[2 * parts + 1]
    rest = list(refs[2 * parts + 2 :])
    kept = [[rest.pop(0) for _ in range(stages - 1)] for _ in range(parts)]
    held = [[rest.pop(0) for _ in range(stages)] for _ in range(parts)]
    gain_held = [rest.pop(0) for _ in range(stages)]
    gain_sum = rest.pop(0)
    send_sem, recv_sem, gain_send, gain_recv = rest

    def partner(axis, coordinate):
        at = dict(place)
        at[axis] = coordinate
        return {"dp": (at["z"] * up + at["y"]) * across + at["x"], "tensor": at["t"]}

    barrier = pltpu.get_barrier_semaphore()
    partners = 0
    for axis, size in extent.items():
        for by in range(1, size):
            partners += 1
            pl.semaphore_signal(
                barrier,
                inc=1,
                device_id=partner(axis, lax.rem(place[axis] + by, size)),
                device_id_type=MESH,
            )
    pl.semaphore_wait(barrier, partners)

    def copies(part, stage):
        axis = orders[part][stage]
        size = extent[axis]
        source = ins[part] if stage == 0 else kept[part][stage - 1]
        blocks = source.shape[0] // size
        made = []
        for by in range(1, size):
            target = lax.rem(place[axis] + by, size)
            made.append(
                pltpu.make_async_remote_copy(
                    src_ref=source.at[pl.ds(target * blocks, blocks)],
                    dst_ref=held[part][stage].at[pl.ds((by - 1) * blocks, blocks)],
                    send_sem=send_sem.at[(part * stages + stage) * steps + by],
                    recv_sem=recv_sem.at[(part * stages + stage) * steps + by],
                    device_id=partner(axis, target),
                    device_id_type=MESH,
                )
            )
        return made

    def gain_copies(stage):
        axis = orders[0][stage]
        size = extent[axis]
        return [
            pltpu.make_async_remote_copy(
                src_ref=gain_ref if stage == 0 else gain_sum.at[stage - 1],
                dst_ref=gain_held[stage].at[place[axis]],
                send_sem=gain_send.at[stage * steps + by],
                recv_sem=gain_recv.at[stage * steps + by],
                device_id=partner(axis, lax.rem(place[axis] + by, size)),
                device_id_type=MESH,
            )
            for by in range(1, size)
        ]

    def start(part, stage):
        for copy in copies(part, stage):
            copy.start()

    def finish(part, stage):
        for copy in copies(part, stage):
            copy.wait_recv()
        axis = orders[part][stage]
        size = extent[axis]
        source = ins[part] if stage == 0 else kept[part][stage - 1]
        blocks = source.shape[0] // size

        def add(block, unused):
            value = source[place[axis] * blocks + block].astype(jnp.float32)
            for by in range(1, size):
                value += held[part][stage][(by - 1) * blocks + block].astype(jnp.float32)
            if stage < stages - 1:
                kept[part][stage][block] = value.astype(jnp.bfloat16)
            else:
                outs[part][...] = value
            return unused

        lax.fori_loop(0, blocks, add, 0)

    def start_gain(stage):
        for copy in gain_copies(stage):
            copy.start()

    def finish_gain(stage):
        axis = orders[0][stage]
        for by, copy in enumerate(gain_copies(stage)):
            copy.wait_recv()
        gain_held[stage][place[axis]] = gain_ref[...] if stage == 0 else gain_sum[stage - 1]
        value = gain_held[stage][0]
        for other in range(1, extent[axis]):
            value += gain_held[stage][other]
        gain_sum[stage] = value

    for part in range(parts):
        start(part, 0)
    start_gain(0)
    for stage in range(stages):
        for part in range(parts):
            finish(part, stage)
            if stage < stages - 1:
                start(part, stage + 1)
        finish_gain(stage)
        if stage < stages - 1:
            start_gain(stage + 1)
    gain_out[...] = gain_sum[stages - 1]
    for stage in range(stages):
        for part in range(parts):
            for copy in copies(part, stage):
                copy.wait_send()
        for copy in gain_copies(stage):
            copy.wait_send()


def directions(count):
    side = round((count // 2) ** (1 / 3))
    if side > 0 and 2 * side * side * side == count:
        return side, side, 2 * side
    return 1, 1, count


def block_order(order, extent, blocks):
    there = []
    for block in range(blocks):
        at, left = {}, block
        for axis in "xyzt":
            at[axis], left = left % extent[axis], left // extent[axis]
        slot = 0
        for axis in order:
            slot = slot * extent[axis] + at[axis]
        there.append(slot)
    return there


def weight_kernel(slots, pair, gqkv_ref, a_ref, go_ref, o_ref, ggate_ref, gup_ref, m_ref, hidden_ref, gy_ref, out_ref, attn_ref):
    bf16 = jnp.bfloat16
    blocks, rows, _ = out_ref.shape
    piece = rows // 4
    chips = blocks // pair
    inward = cols_by_cols(gqkv_ref[...], a_ref[...]).astype(bf16)
    starts = [head * TILE for head in range(H + KV)]
    starts += [(H + head) * TILE + HD for head in range(KV)]
    for place, start in enumerate(starts):
        attn_ref[place * HD : (place + 1) * HD, :] = inward[start : start + HD]
    attn_ref[len(starts) * HD :, :] = cols_by_cols(go_ref[...], o_ref[...]).astype(bf16)
    for block in range(blocks):
        core, chip = block // chips, block % chips
        first = (chip * pair + core) * piece
        out_ref[slots[block], 0:piece, :] = attn_ref[first : first + piece, :]
    grads = ((ggate_ref, m_ref), (gup_ref, m_ref), (hidden_ref, gy_ref))
    for slot, (left, right) in enumerate(grads):
        product = cols_by_cols(left[...], right[...]).astype(bf16)
        for block in range(blocks):
            out_ref[slots[block], (slot + 1) * piece : (slot + 2) * piece, :] = product[
                block * piece : (block + 1) * piece
            ]


def sum_grads(layer_parts, gains):
    bf16 = jnp.bfloat16
    pair = lax.axis_size("tensor")
    across, up, deep = directions(lax.axis_size("dp"))
    extent = {"t": pair, "x": across, "y": up, "z": deep}
    width = gains.shape[1]
    orders = ["txyz" if part % 2 == 0 else "tyxz" for part in range(len(layer_parts))]
    chips = across * up * deep
    stacked = []
    for order, operands in zip(orders, layer_parts):
        gqkv, a, go, o, ggate, gup, m, hidden, gy = operands
        blocks = pair * chips
        piece = hidden.shape[1] // blocks
        if piece % 16 == 0:
            slots = block_order(order, extent, blocks)
            stacked.append(
                call(
                    functools.partial(weight_kernel, tuple(slots), pair),
                    jax.ShapeDtypeStruct((blocks, 4 * piece, width), bf16),
                    [pltpu.VMEM((hidden.shape[1], width), bf16)],
                )(*operands)
            )
            continue
        ffn = [
            cols_by_cols(left, right).astype(bf16)
            for left, right in ((ggate, m), (gup, m), (hidden, gy))
        ]
        g_in = cols_by_cols(gqkv, a).reshape(H + KV, 2, HD, width)
        attn = jnp.concatenate(
            [
                g_in[:H, 0].reshape(H * HD, width),
                g_in[H:, 0].reshape(KV * HD, width),
                g_in[H:, 1].reshape(KV * HD, width),
                cols_by_cols(go, o),
            ],
            axis=0,
        ).astype(bf16)
        split = [jnp.transpose(attn.reshape(chips, pair, piece, width), (1, 0, 2, 3))]
        split += [part.reshape(pair, chips, piece, width) for part in ffn]
        whole = jnp.stack(split, axis=2).reshape(pair, deep, up, across, 4 * piece, width)
        turn = (0, 3, 2, 1, 4, 5) if order == "txyz" else (0, 2, 3, 1, 4, 5)
        stacked.append(jnp.transpose(whole, turn).reshape(blocks, 4 * piece, width))
    rows = stacked[0].shape[1]
    stages = 4
    kept, held = [], []
    for order in orders:
        blocks = pair * chips
        for stage, axis in enumerate(order):
            blocks //= extent[axis]
            if stage < stages - 1:
                kept.append(pltpu.VMEM((blocks, rows, width), bf16))
            held.append(
                pltpu.VMEM((max(extent[axis] - 1, 1) * blocks, rows, width), bf16)
            )
    gain_held = [pltpu.VMEM((extent[axis],) + gains.shape, jnp.float32) for axis in orders[0]]
    steps = max(extent.values())
    slots = len(orders) * stages * steps
    *sums, gain_sums = call(
        functools.partial(sum_kernel, (pair, across, up, deep), tuple(orders)),
        tuple(jax.ShapeDtypeStruct((rows, width), jnp.float32) for _ in orders)
        + (jax.ShapeDtypeStruct(gains.shape, jnp.float32),),
        kept
        + held
        + gain_held
        + [
            pltpu.VMEM((stages,) + gains.shape, jnp.float32),
            pltpu.SemaphoreType.DMA((slots,)),
            pltpu.SemaphoreType.DMA((slots,)),
            pltpu.SemaphoreType.DMA((stages * steps,)),
            pltpu.SemaphoreType.DMA((stages * steps,)),
        ],
        collective_id=2,
        has_side_effects=True,
    )(*stacked, gains)
    return [jnp.split(value, 4, axis=0) for value in sums], gain_sums


def body(tokens, w_attn, attn_gain, w_gate, w_up, w_down, mlp_gain, seq_lengths, cotangent):
    own, width = tokens.shape
    layers = w_attn.shape[0]
    count = lax.axis_size("dp") * lax.axis_size("tensor")
    qkv_rows = (H + 2 * KV) * HD
    reach = (L_MAX + own - 2) // own
    reach += 1 - reach % 2
    window_rows = (reach + 1) * own
    chunk_rows = 2 * own if (reach + 1) % 2 == 0 else own
    tiles = (H + KV) * TILE
    f32, bf16 = jnp.float32, jnp.bfloat16
    shape = jax.ShapeDtypeStruct

    seq_ends = jnp.cumsum(seq_lengths)
    starts = seq_ends - seq_lengths
    first_place = lax.axis_index(AXES) * own
    places = first_place + jnp.arange(own, dtype=jnp.int32)
    begin = sequence_start(places, starts)
    first_key = first_place - reach * own
    low = jnp.tile(begin - first_key, GROUPS)[None, :]
    high = jnp.tile(places - first_key, GROUPS)[None, :]
    frequencies = jnp.power(ROPE_BASE, -2.0 * jnp.arange(HD // 2, dtype=f32) / HD)
    angles = (places - begin).astype(f32)[:, None] * frequencies[None, :]
    cosines, sines = jnp.cos(angles), jnp.sin(angles)
    zeros, ones = jnp.zeros((own, HD), f32), jnp.ones((own, HD), f32)
    cos_q = jnp.concatenate([cosines, cosines, zeros], axis=1)
    cos_kv = jnp.concatenate([cosines, cosines, ones], axis=1)
    sin_all = jnp.concatenate([-sines, sines, zeros], axis=1)

    gate_all = lax.all_gather(w_gate, "tensor", axis=1, tiled=True)
    up_all = lax.all_gather(w_up, "tensor", axis=1, tiled=True)
    down_all = lax.all_gather(w_down, "tensor", axis=1, tiled=True)
    q_rows = w_attn[:, : H * HD].reshape(layers, H, HD, width)
    k_rows = w_attn[:, H * HD : (H + KV) * HD].reshape(layers, KV, HD, width)
    v_rows = w_attn[:, (H + KV) * HD : qkv_rows].reshape(layers, KV, HD, width)
    w_in = jnp.concatenate(
        [
            jnp.pad(q_rows, ((0, 0), (0, 0), (0, HD), (0, 0))),
            jnp.concatenate([k_rows, v_rows], axis=2),
        ],
        axis=1,
    ).reshape(layers, tiles, width)
    w_out = jnp.pad(
        jnp.swapaxes(w_attn[:, qkv_rows:], 1, 2).reshape(layers, H, HD, width),
        ((0, 0), (0, 0), (HD, 0), (0, 0)),
    )

    stream = tokens.astype(f32)
    stored = []
    for layer in range(layers):
        queries, kv_own, normed = call(
            project_kernel,
            (
                shape((KV, GROUPS * own, TILE), bf16),
                shape((own, KV * TILE), bf16),
                shape((own, width), bf16),
            ),
        )(stream, attn_gain[layer][None], w_in[layer], cos_q, cos_kv, sin_all)
        window = call(
            functools.partial(fetch_kernel, count, reach),
            shape((reach + 1, own, KV * TILE), bf16),
            [pltpu.SemaphoreType.DMA((reach + 1,)) for _ in range(3)],
            collective_id=0,
            has_side_effects=True,
        )(kv_own).reshape(window_rows, KV * TILE)
        hidden_rows = gate_all.shape[1]
        x_out, middle, normed_m, gate, up, hidden, mixed, lse = call(
            functools.partial(attend_kernel, chunk_rows),
            (
                shape((own, width), f32),
                shape((own, width), f32),
                shape((own, width), bf16),
                shape((own, hidden_rows), f32),
                shape((own, hidden_rows), f32),
                shape((own, hidden_rows), bf16),
                shape((KV, GROUPS * own, TILE), f32),
                shape((KV, 1, GROUPS * own), f32),
            ),
            [
                pltpu.VMEM((KV, TILE, GROUPS * own), f32),
                pltpu.VMEM((KV, 1, GROUPS * own), f32),
                pltpu.VMEM((KV, 1, GROUPS * own), f32),
            ],
        )(
            queries,
            window,
            low,
            high,
            stream,
            w_out[layer],
            mlp_gain[layer][None],
            gate_all[layer],
            up_all[layer],
            down_all[layer],
        )
        stored.append((stream, queries, normed, window, middle, normed_m, gate, up, hidden, mixed, lse))
        stream = x_out

    upstream = cotangent
    gains = []
    parts = []
    for layer in reversed(range(layers)):
        x_in, queries, normed, window, middle, normed_m, gate, up, hidden, mixed, lse = stored[layer]
        hidden_rows = gate_all.shape[1]
        gy, ggate, gup, gmid, go, gain_m = call(
            mlp_back_kernel,
            (
                shape((own, width), bf16),
                shape((own, hidden_rows), bf16),
                shape((own, hidden_rows), bf16),
                shape((own, width), f32),
                shape((own, width), bf16),
                shape((1, width), f32),
            ),
        )(
            upstream,
            middle,
            gate,
            up,
            mlp_gain[layer][None],
            gate_all[layer],
            up_all[layer],
            down_all[layer],
        )
        heads = jnp.transpose(
            mixed.reshape(H, own, TILE)[:, :, HD:].astype(bf16), (1, 0, 2)
        ).reshape(own, H * HD)
        gq, gwin = call(
            functools.partial(attend_back_kernel, chunk_rows),
            (
                shape((KV, GROUPS * own, TILE), f32),
                shape((window_rows, KV * TILE), bf16),
            ),
            [
                pltpu.VMEM((KV, GROUPS * own, TILE), bf16),
                pltpu.VMEM((KV, 1, GROUPS * own), f32),
                pltpu.VMEM((KV, TILE, GROUPS * own), f32),
            ],
        )(go, w_out[layer], queries, window, low, high, mixed, lse)
        gkv = call(
            functools.partial(return_kernel, count, reach),
            shape((own, KV * TILE), f32),
            [
                pltpu.VMEM((reach // 2 + 1, own, KV * TILE), bf16),
                pltpu.VMEM((reach // 2, own, KV * TILE), bf16),
                pltpu.VMEM((reach // 2 + 1, own, KV * TILE), bf16),
            ]
            + [pltpu.SemaphoreType.DMA((reach + 1,)) for _ in range(4)],
            collective_id=1,
            has_side_effects=True,
        )(gwin.reshape(reach + 1, own, KV * TILE))
        gqkv, upstream, gain_a = call(
            project_back_kernel,
            (
                shape((own, tiles), bf16),
                shape((own, width), f32),
                shape((1, width), f32),
            ),
        )(gq, gkv, cos_q, cos_kv, sin_all, w_in[layer], x_in, attn_gain[layer][None], gmid)
        gains.append((gain_a, gain_m))

        parts.append([gqkv, normed, go, heads, ggate, gup, normed_m, hidden, gy])
    rows = [row for pair in gains[::-1] for row in pair]
    rows.append(jnp.zeros((-len(rows) % 8, width), f32))
    sums, gain_sums = sum_grads(parts[::-1], jnp.concatenate(rows, axis=0))
    attn_sum, gate_sum, up_sum, down_sum = [
        jnp.stack([entry[slot] for entry in sums], axis=0) for slot in range(4)
    ]
    gain_sums = gain_sums[: 2 * layers]
    return (
        stream,
        upstream,
        attn_sum,
        gain_sums[0::2],
        gate_sum,
        up_sum,
        down_sum,
        gain_sums[1::2],
    )


def solution(mesh):
    placed = (
        P(AXES, None),
        P(),
        P(),
        P(None, "tensor", None),
        P(None, "tensor", None),
        P(None, "tensor", None),
        P(),
        P(),
        P(AXES, None),
    )
    return jax.shard_map(
        body,
        mesh=mesh,
        in_specs=placed,
        out_specs=(
            P(AXES, None),
            P(AXES, None),
            P(None, AXES, None),
            P(),
            P(None, ("tensor", "dp"), None),
            P(None, ("tensor", "dp"), None),
            P(None, ("tensor", "dp"), None),
            P(),
        ),
        check_vma=False,
    )
```

```python
import functools

import jax
import jax.numpy as jnp
from jax import lax
from jax.experimental import pallas as pl
from jax.experimental.pallas import tpu as pltpu
from jax.sharding import PartitionSpec as P

H = 9
KV = 3
GROUPS = H // KV
HD = 64
TILE = 2 * HD
L_MAX = 2048

EPSILON = 1e-05
ROPE_BASE = 100000.0
MASKED = -1e30
MESH = pl.DeviceIdType.MESH
AXES = ("dp", "tensor")
VMEM_LIMIT = 56 * 1024 * 1024


def rows_by_rows(left, right):
    return lax.dot_general(
        left, right, (((1,), (1,)), ((), ())), preferred_element_type=jnp.float32
    )


def cols_by_cols(left, right):
    return lax.dot_general(
        left, right, (((0,), (0,)), ((), ())), preferred_element_type=jnp.float32
    )


def plain_dot(left, right):
    return jnp.dot(left, right, preferred_element_type=jnp.float32)


def sequence_start(places, starts):
    reached = starts[None, :] <= places[:, None]
    return jnp.max(jnp.where(reached, starts[None, :], -1), axis=1)


def rms_parts(values):
    inverse = lax.rsqrt(jnp.mean(values * values, axis=-1, keepdims=True) + EPSILON)
    return (values * inverse, inverse)


def norm_back(grad_out, ratio, inverse, gain_vec):
    scaled = grad_out * gain_vec
    input_grad = inverse * (scaled - ratio * jnp.mean(scaled * ratio, axis=-1, keepdims=True))
    return (input_grad, jnp.sum(grad_out * ratio, axis=0, keepdims=True))


def swap_halves(values):
    lane = lax.broadcasted_iota(jnp.int32, values.shape, 1)
    return jnp.where(
        lane < HD // 2,
        pltpu.roll(values, TILE - HD // 2, 1),
        pltpu.roll(values, HD // 2, 1),
    )


def call(kernel, out_shape, scratch=(), specs=None, **params):
    given = {}
    if specs is not None:
        given = {"grid": (1,), "in_specs": specs, "out_specs": tuple(whole_spec() for _ in out_shape)}
    return pl.pallas_call(
        kernel,
        out_shape=out_shape,
        **given,
        scratch_shapes=list(scratch),
        compiler_params=pltpu.CompilerParams(vmem_limit_bytes=VMEM_LIMIT, **params),
    )


def whole_spec():
    return pl.BlockSpec(memory_space=pltpu.VMEM)


def attn_spec(w_attn, layer):
    return pl.BlockSpec((None,) + w_attn.shape[1:], lambda step: (layer, 0, 0))


def ffn_spec(weights, layer):
    pair, _, rows, width = weights.shape
    return pl.BlockSpec((pair, None, rows, width), lambda step: (0, layer, 0, 0))


def joined_rows(ref):
    value = ref[...]
    return value.reshape(value.shape[0] * value.shape[1], value.shape[2])


def spread_rows(wide_ref, w_ref):
    for head in range(H + KV):
        start = head * TILE
        wide_ref[start : start + HD, :] = w_ref[head * HD : (head + 1) * HD, :]
        if head < H:
            wide_ref[start + HD : start + TILE, :] = jnp.zeros(
                (HD, wide_ref.shape[1]), wide_ref.dtype
            )
        else:
            value = (head + KV) * HD
            wide_ref[start + HD : start + TILE, :] = w_ref[value : value + HD, :]


def project_kernel(x_ref, gain_ref, w_ref, cq_ref, ckv_ref, sn_ref, q_ref, kv_ref, a_ref, wide_ref):
    own = x_ref.shape[0]
    spread_rows(wide_ref, w_ref)
    ratio, _ = rms_parts(x_ref[...])
    normed = (ratio * gain_ref[...]).astype(jnp.bfloat16)
    a_ref[...] = normed
    sines = sn_ref[...]
    for head in range(H + KV):
        lin = rows_by_rows(normed, wide_ref[head * TILE : (head + 1) * TILE, :])
        cosines = cq_ref[...] if head < H else ckv_ref[...]
        turned = (lin * cosines + swap_halves(lin) * sines).astype(jnp.bfloat16)
        if head < H:
            rows = slice((head % GROUPS) * own, (head % GROUPS + 1) * own)
            q_ref[head // GROUPS, rows, :] = turned * jnp.bfloat16(0.125)
        else:
            kv_ref[:, (head - H) * TILE : (head - H + 1) * TILE] = turned


def mesh_id(index, pair):
    return {"dp": lax.div(index, pair), "tensor": lax.rem(index, pair)}


def greet(me, count, reach, step, senders_pair, copies_pair):
    barrier = pltpu.get_barrier_semaphore()
    core = lax.rem(me, 2)
    far_sender = 0 if step < 0 else 1
    waits = jnp.where(copies_pair, 1, 0)
    for by in list(range(2, reach, 2)) + [reach]:
        sender, target = me + step * by, me - step * by
        hears = (sender >= 0) & (sender < count)
        sends = (target >= 0) & (target < count)
        if by == reach:
            hears = hears & (core == far_sender)
            sends = sends & (core == 1 - far_sender)

        @pl.when(hears)
        def _():
            pl.semaphore_signal(
                barrier, inc=1, device_id=mesh_id(sender, 2), device_id_type=MESH
            )

        waits = waits + jnp.where(sends, 1, 0)

    @pl.when(senders_pair)
    def _():
        pl.semaphore_signal(
            barrier, inc=1, device_id=mesh_id(me + 1 - 2 * core, 2), device_id_type=MESH
        )

    @pl.when(waits > 0)
    def _():
        pl.semaphore_wait(barrier, waits)


def fetch_kernel(count, reach, own_ref, window_ref, send_sem, recv_sem, pass_sem):
    core = lax.axis_index("tensor")
    me = lax.axis_index("dp") * 2 + core
    sibling = me + 1 - 2 * core
    greet(me, count, reach, -1, (core == 1) | (me > 0), (core == 0) | (me > 1))

    def send(by):
        return pltpu.make_async_remote_copy(
            src_ref=own_ref,
            dst_ref=window_ref.at[reach - by],
            send_sem=send_sem.at[by],
            recv_sem=recv_sem.at[by],
            device_id=mesh_id(me + by, 2),
            device_id_type=MESH,
        )

    def hand_over(by):
        there = by + 1 - 2 * core
        return pltpu.make_async_remote_copy(
            src_ref=own_ref if by == 0 else window_ref.at[reach - by],
            dst_ref=window_ref.at[reach - there],
            send_sem=pass_sem.at[by],
            recv_sem=recv_sem.at[there],
            device_id=mesh_id(sibling, 2),
            device_id_type=MESH,
        )

    even = list(range(2, reach, 2))
    for by in even:

        @pl.when(me + by < count)
        def _():
            send(by).start()

    @pl.when((core == 1) & (me + reach < count))
    def _():
        send(reach).start()

    @pl.when(core == 0)
    def _():
        hand_over(0).start()

    window_ref[reach] = own_ref[...]
    for by in range(1, reach + 1):

        @pl.when(me - by < 0)
        def _():
            window_ref[reach - by] = jnp.zeros(own_ref.shape, own_ref.dtype)

    for by in even:

        @pl.when(me - by >= 0)
        def _():
            send(by).wait_recv()
            hand_over(by).start()

    for by in range(1, reach + 1, 2):

        @pl.when(me - by >= 0)
        def _():
            send(by).wait_recv()

    for by in even:

        @pl.when(me - by >= 0)
        def _():
            hand_over(by).wait_send()

        @pl.when(me + by < count)
        def _():
            send(by).wait_send()

    @pl.when((core == 1) & (me + reach < count))
    def _():
        send(reach).wait_send()

    @pl.when(core == 0)
    def _():
        hand_over(0).wait_send()


def return_kernel(
    count, reach, grads_ref, sum_ref, near, joined, held, send_sem, recv_sem, pass_sem, near_sem
):
    core = lax.axis_index("tensor")
    me = lax.axis_index("dp") * 2 + core
    sibling = me + 1 - 2 * core
    greet(me, count, reach, 1, (core == 0) | (me > 1), (core == 1) | (me > 0))
    even = list(range(2, reach, 2))

    def hand_over(by):
        slot = (by + 1) // 2 - core
        return pltpu.make_async_remote_copy(
            src_ref=grads_ref.at[reach - by],
            dst_ref=near.at[slot],
            send_sem=pass_sem.at[by],
            recv_sem=near_sem.at[slot],
            device_id=mesh_id(sibling, 2),
            device_id_type=MESH,
        )

    def taken(slot):
        return pltpu.make_async_remote_copy(
            src_ref=grads_ref.at[0],
            dst_ref=near.at[slot],
            send_sem=pass_sem.at[0],
            recv_sem=near_sem.at[slot],
            device_id=mesh_id(sibling, 2),
            device_id_type=MESH,
        )

    def send(by):
        return pltpu.make_async_remote_copy(
            src_ref=grads_ref.at[0] if by == reach else joined.at[by // 2 - 1],
            dst_ref=held.at[by // 2 - 1 + by % 2],
            send_sem=send_sem.at[by],
            recv_sem=recv_sem.at[by],
            device_id=mesh_id(me - by, 2),
            device_id_type=MESH,
        )

    @pl.when((core == 0) & (me - reach >= 0))
    def _():
        send(reach).start()

    for by in range(reach, 0, -2):
        wanted = me - by >= 0
        if by == reach:
            wanted = wanted & (core == 1)

        @pl.when(wanted)
        def _():
            hand_over(by).start()

    for by in even[::-1]:

        @pl.when(me - by >= 0)
        def _():
            taken(by // 2).wait_recv()
            joined[by // 2 - 1] = (
                grads_ref[reach - by].astype(jnp.float32) + near[by // 2].astype(jnp.float32)
            ).astype(jnp.bfloat16)
            send(by).start()

    sum_ref[...] = grads_ref[reach].astype(jnp.float32)

    @pl.when(core == 0)
    def _():
        taken(0).wait_recv()
        sum_ref[...] += near[0].astype(jnp.float32)

    for by in even + [reach]:
        comes = me + by < count
        if by == reach:
            comes = comes & (core == 1)

        @pl.when(comes)
        def _():
            send(by).wait_recv()
            sum_ref[...] += held[by // 2 - 1 + by % 2].astype(jnp.float32)

    for by in even:

        @pl.when(me - by >= 0)
        def _():
            send(by).wait_send()

    @pl.when((core == 0) & (me - reach >= 0))
    def _():
        send(reach).wait_send()

    for by in range(reach, 0, -2):
        wanted = me - by >= 0
        if by == reach:
            wanted = wanted & (core == 1)

        @pl.when(wanted)
        def _():
            hand_over(by).wait_send()


def allowed_pairs(chunk, rows, low_ref, high_ref):
    place = chunk * rows + lax.broadcasted_iota(jnp.int32, (rows, low_ref.shape[1]), 0)
    return (place >= low_ref[...]) & (place <= high_ref[...])


def attend_kernel(
    chunk_rows,
    q_ref,
    win_ref,
    low_ref,
    high_ref,
    x_ref,
    wo_ref,
    gain_ref,
    wg_ref,
    wu_ref,
    wd_ref,
    x_out_ref,
    mid_ref,
    m_ref,
    gate_ref,
    up_ref,
    hidden_ref,
    o_ref,
    lse_ref,
    acc_ref,
    top_ref,
    total_ref,
):
    own = x_ref.shape[0]
    chunks = win_ref.shape[0] // chunk_rows
    acc_ref[...] = jnp.zeros_like(acc_ref)
    total_ref[...] = jnp.zeros_like(total_ref)
    top_ref[...] = jnp.full_like(top_ref, MASKED)

    def step(chunk, unused):
        allowed = allowed_pairs(chunk, chunk_rows, low_ref, high_ref)
        start = pl.multiple_of(chunk * chunk_rows, chunk_rows)
        for j in range(KV):
            tile = win_ref[pl.ds(start, chunk_rows), j * TILE : (j + 1) * TILE]
            scores = jnp.where(allowed, rows_by_rows(tile, q_ref[j]), MASKED)
            highest = top_ref[j]
            newest = jnp.maximum(highest, jnp.max(scores, axis=0, keepdims=True))
            terms = jnp.exp(scores - newest)
            decay = jnp.exp(highest - newest)
            top_ref[j] = newest
            total_ref[j] = total_ref[j] * decay + jnp.sum(terms, axis=0, keepdims=True)
            acc_ref[j] = acc_ref[j] * decay + cols_by_cols(tile, terms.astype(jnp.bfloat16))
        return unused

    lax.fori_loop(0, chunks, step, 0)
    middle = x_ref[...]
    for j in range(KV):
        lse_ref[j] = top_ref[j] + jnp.log(total_ref[j])
        mixed = (acc_ref[j] / total_ref[j]).T
        o_ref[j] = mixed
        low = mixed.astype(jnp.bfloat16)
        for g in range(GROUPS):
            middle = middle + plain_dot(low[g * own : (g + 1) * own], wo_ref[j * GROUPS + g])
    mid_ref[...] = middle
    ratio, _ = rms_parts(middle)
    normed = (ratio * gain_ref[...]).astype(jnp.bfloat16)
    m_ref[...] = normed
    gate = rows_by_rows(normed, joined_rows(wg_ref))
    up = rows_by_rows(normed, joined_rows(wu_ref))
    gate_ref[...] = gate
    up_ref[...] = up
    hidden = (gate * jax.nn.sigmoid(gate) * up).astype(jnp.bfloat16)
    hidden_ref[...] = hidden
    x_out_ref[...] = middle + plain_dot(hidden, joined_rows(wd_ref))


def mlp_back_kernel(
    gx_ref,
    mid_ref,
    gate_ref,
    up_ref,
    gain_ref,
    wg_ref,
    wu_ref,
    wd_ref,
    gy_ref,
    ggate_ref,
    gup_ref,
    gmid_ref,
    go_ref,
    ggain_ref,
):
    gx = gx_ref[...].astype(jnp.float32)
    gy = gx.astype(jnp.bfloat16)
    gy_ref[...] = gy
    gh = rows_by_rows(gy, joined_rows(wd_ref))
    gate = gate_ref[...]
    sig = jax.nn.sigmoid(gate)
    ggate = (gh * up_ref[...] * sig * (1.0 + gate * (1.0 - sig))).astype(jnp.bfloat16)
    gup = (gh * gate * sig).astype(jnp.bfloat16)
    ggate_ref[...] = ggate
    gup_ref[...] = gup
    gm = plain_dot(ggate, joined_rows(wg_ref)) + plain_dot(gup, joined_rows(wu_ref))
    ratio, inverse = rms_parts(mid_ref[...])
    back, ggain = norm_back(gm, ratio, inverse, gain_ref[...])
    ggain_ref[...] = ggain
    gmid = gx + back
    gmid_ref[...] = gmid
    go_ref[...] = gmid.astype(jnp.bfloat16)


def attend_back_kernel(
    chunk_rows,
    go_ref,
    wo_ref,
    q_ref,
    win_ref,
    low_ref,
    high_ref,
    o_ref,
    lse_ref,
    gq_ref,
    gwin_ref,
    grad_ref,
    delta_ref,
    acc_ref,
):
    own = go_ref.shape[0]
    chunks = win_ref.shape[0] // chunk_rows
    go = go_ref[...]
    lane = lax.broadcasted_iota(jnp.int32, (GROUPS * own, TILE), 1)
    for j in range(KV):
        for g in range(GROUPS):
            grad_ref[j, g * own : (g + 1) * own, :] = rows_by_rows(
                go, wo_ref[j * GROUPS + g]
            ).astype(jnp.bfloat16)
        product = jnp.where(lane >= HD, grad_ref[j].astype(jnp.float32) * o_ref[j], 0.0)
        delta_ref[j] = jnp.sum(product.T, axis=0, keepdims=True)
    acc_ref[...] = jnp.zeros_like(acc_ref)

    def step(chunk, unused):
        allowed = allowed_pairs(chunk, chunk_rows, low_ref, high_ref)
        start = pl.multiple_of(chunk * chunk_rows, chunk_rows)
        for j in range(KV):
            tile = win_ref[pl.ds(start, chunk_rows), j * TILE : (j + 1) * TILE]
            queries = q_ref[j]
            grads = grad_ref[j]
            scores = rows_by_rows(tile, queries) - lse_ref[j]
            weights = jnp.exp(jnp.where(allowed, scores, MASKED))
            slopes = rows_by_rows(tile, grads) - delta_ref[j]
            score_grads = (weights * slopes).astype(jnp.bfloat16)
            acc_ref[j] += cols_by_cols(tile, score_grads)
            both = plain_dot(score_grads, queries) + plain_dot(
                weights.astype(jnp.bfloat16), grads
            )
            gwin_ref[pl.ds(start, chunk_rows), j * TILE : (j + 1) * TILE] = both.astype(
                jnp.bfloat16
            )
        return unused

    lax.fori_loop(0, chunks, step, 0)
    for j in range(KV):
        gq_ref[j] = (0.125 * acc_ref[j]).T


def project_back_kernel(
    gq_ref, gkv_ref, cq_ref, ckv_ref, sn_ref, w_ref, x_ref, gain_ref, gmid_ref, gqkv_ref, gx_ref, ggain_ref, wide_ref
):
    own = x_ref.shape[0]
    spread_rows(wide_ref, w_ref)
    sines = -sn_ref[...]
    for head in range(H + KV):
        if head < H:
            rows = slice((head % GROUPS) * own, (head % GROUPS + 1) * own)
            lin = gq_ref[head // GROUPS, rows, :]
            cosines = cq_ref[...]
        else:
            lin = gkv_ref[:, (head - H) * TILE : (head - H + 1) * TILE]
            cosines = ckv_ref[...]
        turned = (lin * cosines + swap_halves(lin) * sines).astype(jnp.bfloat16)
        gqkv_ref[:, head * TILE : (head + 1) * TILE] = turned
    grad_normed = plain_dot(gqkv_ref[...], wide_ref[...])
    ratio, inverse = rms_parts(x_ref[...])
    back, ggain = norm_back(grad_normed, ratio, inverse, gain_ref[...])
    ggain_ref[...] = ggain
    gx_ref[...] = gmid_ref[...] + back


def sum_kernel(sizes, orders, *refs):
    parts = len(orders)
    pair, across, up, deep = sizes
    core = lax.axis_index("tensor")
    index = lax.axis_index("dp")
    place = {
        "t": core,
        "x": lax.rem(index, across),
        "y": lax.rem(lax.div(index, across), up),
        "z": lax.div(index, across * up),
    }
    extent = {"t": pair, "x": across, "y": up, "z": deep}
    stages = len(orders[0])
    steps = max(extent.values())
    ins, gain_ref = refs[:parts], refs[parts]
    outs, gain_out = refs[parts + 1 : 2 * parts + 1], refs[2 * parts + 1]
    rest = list(refs[2 * parts + 2 :])
    kept = [[rest.pop(0) for _ in range(stages - 1)] for _ in range(parts)]
    held = [[rest.pop(0) for _ in range(stages)] for _ in range(parts)]
    gain_held = [rest.pop(0) for _ in range(stages)]
    gain_sum = rest.pop(0)
    send_sem, recv_sem, gain_send, gain_recv = rest

    def partner(axis, coordinate):
        at = dict(place)
        at[axis] = coordinate
        return {"dp": (at["z"] * up + at["y"]) * across + at["x"], "tensor": at["t"]}

    barrier = pltpu.get_barrier_semaphore()
    partners = 0
    for axis, size in extent.items():
        for by in range(1, size):
            partners += 1
            pl.semaphore_signal(
                barrier,
                inc=1,
                device_id=partner(axis, lax.rem(place[axis] + by, size)),
                device_id_type=MESH,
            )
    pl.semaphore_wait(barrier, partners)

    def copies(part, stage):
        axis = orders[part][stage]
        size = extent[axis]
        source = ins[part] if stage == 0 else kept[part][stage - 1]
        blocks = source.shape[0] // size
        made = []
        for by in range(1, size):
            target = lax.rem(place[axis] + by, size)
            made.append(
                pltpu.make_async_remote_copy(
                    src_ref=source.at[pl.ds(target * blocks, blocks)],
                    dst_ref=held[part][stage].at[pl.ds((by - 1) * blocks, blocks)],
                    send_sem=send_sem.at[(part * stages + stage) * steps + by],
                    recv_sem=recv_sem.at[(part * stages + stage) * steps + by],
                    device_id=partner(axis, target),
                    device_id_type=MESH,
                )
            )
        return made

    def gain_copies(stage):
        axis = orders[0][stage]
        size = extent[axis]
        return [
            pltpu.make_async_remote_copy(
                src_ref=gain_ref if stage == 0 else gain_sum.at[stage - 1],
                dst_ref=gain_held[stage].at[place[axis]],
                send_sem=gain_send.at[stage * steps + by],
                recv_sem=gain_recv.at[stage * steps + by],
                device_id=partner(axis, lax.rem(place[axis] + by, size)),
                device_id_type=MESH,
            )
            for by in range(1, size)
        ]

    def start(part, stage):
        for copy in copies(part, stage):
            copy.start()

    def finish(part, stage):
        for copy in copies(part, stage):
            copy.wait_recv()
        axis = orders[part][stage]
        size = extent[axis]
        source = ins[part] if stage == 0 else kept[part][stage - 1]
        blocks = source.shape[0] // size

        def add(block, unused):
            value = source[place[axis] * blocks + block].astype(jnp.float32)
            for by in range(1, size):
                value += held[part][stage][(by - 1) * blocks + block].astype(jnp.float32)
            if stage < stages - 1:
                kept[part][stage][block] = value.astype(jnp.bfloat16)
            else:
                outs[part][...] = value
            return unused

        lax.fori_loop(0, blocks, add, 0)

    def start_gain(stage):
        for copy in gain_copies(stage):
            copy.start()

    def finish_gain(stage):
        axis = orders[0][stage]
        for by, copy in enumerate(gain_copies(stage)):
            copy.wait_recv()
        gain_held[stage][place[axis]] = gain_ref[...] if stage == 0 else gain_sum[stage - 1]
        value = gain_held[stage][0]
        for other in range(1, extent[axis]):
            value += gain_held[stage][other]
        gain_sum[stage] = value

    def start_group(group):
        for part in range(2 * group, 2 * group + 2):
            start(part, 0)

    groups = parts // 2
    start_group(0)
    start_gain(0)
    for step in range(stages + groups - 1):
        for group in range(groups):
            stage = step - group
            if not 0 <= stage < stages:
                continue
            for part in range(2 * group, 2 * group + 2):
                finish(part, stage)
                if stage < stages - 1:
                    start(part, stage + 1)
            if stage == 0 and group < groups - 1:
                start_group(group + 1)
        if step < stages:
            finish_gain(step)
            if step < stages - 1:
                start_gain(step + 1)
    gain_out[...] = gain_sum[stages - 1]
    for stage in range(stages):
        for part in range(parts):
            for copy in copies(part, stage):
                copy.wait_send()
        for copy in gain_copies(stage):
            copy.wait_send()


def directions(count):
    side = round((count // 2) ** (1 / 3))
    if side > 0 and 2 * side * side * side == count:
        return side, side, 2 * side
    return 1, 1, count


def block_order(order, extent, blocks):
    there = []
    for block in range(blocks):
        at, left = {}, block
        for axis in "xyzt":
            at[axis], left = left % extent[axis], left // extent[axis]
        slot = 0
        for axis in order:
            slot = slot * extent[axis] + at[axis]
        there.append(slot)
    return there


def weight_kernel(slots, pair, gqkv_ref, a_ref, go_ref, o_ref, ggate_ref, gup_ref, m_ref, hidden_ref, gy_ref, out_ref, late_ref, attn_ref):
    bf16 = jnp.bfloat16
    blocks, rows, _ = out_ref.shape
    piece = rows // 2
    chips = blocks // pair
    inward = cols_by_cols(gqkv_ref[...], a_ref[...]).astype(bf16)
    starts = [head * TILE for head in range(H + KV)]
    starts += [(H + head) * TILE + HD for head in range(KV)]
    for place, start in enumerate(starts):
        attn_ref[place * HD : (place + 1) * HD, :] = inward[start : start + HD]
    attn_ref[len(starts) * HD :, :] = cols_by_cols(go_ref[...], o_ref[...]).astype(bf16)
    for block in range(blocks):
        core, chip = block // chips, block % chips
        first = (chip * pair + core) * piece
        out_ref[slots[block], 0:piece, :] = attn_ref[first : first + piece, :]
    grads = ((ggate_ref, m_ref), (gup_ref, m_ref), (hidden_ref, gy_ref))
    for slot, (left, right) in enumerate(grads):
        product = cols_by_cols(left[...], right[...]).astype(bf16)
        for block in range(blocks):
            where, half = (out_ref, 1) if slot == 0 else (late_ref, slot - 1)
            where[slots[block], half * piece : (half + 1) * piece, :] = product[
                block * piece : (block + 1) * piece
            ]


def sum_grads(layer_parts, gains):
    bf16 = jnp.bfloat16
    pair = lax.axis_size("tensor")
    across, up, deep = directions(lax.axis_size("dp"))
    extent = {"t": pair, "x": across, "y": up, "z": deep}
    width = gains.shape[1]
    orders = ["txyz" if part % 2 == 0 else "tyxz" for part in range(len(layer_parts))]
    chips = across * up * deep
    stacked = []
    for order, operands in zip(orders, layer_parts):
        gqkv, a, go, o, ggate, gup, m, hidden, gy = operands
        blocks = pair * chips
        piece = hidden.shape[1] // blocks
        if piece % 16 == 0:
            slots = block_order(order, extent, blocks)
            stacked.append(
                call(
                    functools.partial(weight_kernel, tuple(slots), pair),
                    (jax.ShapeDtypeStruct((blocks, 2 * piece, width), bf16),) * 2,
                    [pltpu.VMEM((hidden.shape[1], width), bf16)],
                )(*operands)
            )
            continue
        ffn = [
            cols_by_cols(left, right).astype(bf16)
            for left, right in ((ggate, m), (gup, m), (hidden, gy))
        ]
        g_in = cols_by_cols(gqkv, a).reshape(H + KV, 2, HD, width)
        attn = jnp.concatenate(
            [
                g_in[:H, 0].reshape(H * HD, width),
                g_in[H:, 0].reshape(KV * HD, width),
                g_in[H:, 1].reshape(KV * HD, width),
                cols_by_cols(go, o),
            ],
            axis=0,
        ).astype(bf16)
        split = [jnp.transpose(attn.reshape(chips, pair, piece, width), (1, 0, 2, 3))]
        split += [part.reshape(pair, chips, piece, width) for part in ffn]
        whole = jnp.stack(split, axis=2).reshape(pair, deep, up, across, 4 * piece, width)
        turn = (0, 3, 2, 1, 4, 5) if order == "txyz" else (0, 2, 3, 1, 4, 5)
        stacked.append(
            jnp.split(jnp.transpose(whole, turn).reshape(blocks, 4 * piece, width), 2, axis=1)
        )
    layers = len(stacked)
    stacked = [halves[half] for half in range(2) for halves in stacked]
    orders = orders * 2
    rows = stacked[0].shape[1]
    stages = 4
    kept, held = [], []
    for order in orders:
        blocks = pair * chips
        for stage, axis in enumerate(order):
            blocks //= extent[axis]
            if stage < stages - 1:
                kept.append(pltpu.VMEM((blocks, rows, width), bf16))
            held.append(
                pltpu.VMEM((max(extent[axis] - 1, 1) * blocks, rows, width), bf16)
            )
    gain_held = [pltpu.VMEM((extent[axis],) + gains.shape, jnp.float32) for axis in orders[0]]
    steps = max(extent.values())
    slots = len(orders) * stages * steps
    *sums, gain_sums = call(
        functools.partial(sum_kernel, (pair, across, up, deep), tuple(orders)),
        tuple(jax.ShapeDtypeStruct((rows, width), jnp.float32) for _ in orders)
        + (jax.ShapeDtypeStruct(gains.shape, jnp.float32),),
        kept
        + held
        + gain_held
        + [
            pltpu.VMEM((stages,) + gains.shape, jnp.float32),
            pltpu.SemaphoreType.DMA((slots,)),
            pltpu.SemaphoreType.DMA((slots,)),
            pltpu.SemaphoreType.DMA((stages * steps,)),
            pltpu.SemaphoreType.DMA((stages * steps,)),
        ],
        collective_id=2,
        has_side_effects=True,
    )(*stacked, gains)
    halves = [jnp.split(value, 2, axis=0) for value in sums]
    return [halves[layer] + halves[layers + layer] for layer in range(layers)], gain_sums


def body(tokens, w_attn, attn_gain, w_gate, w_up, w_down, mlp_gain, seq_lengths, cotangent):
    own, width = tokens.shape
    layers = w_attn.shape[0]
    count = lax.axis_size("dp") * lax.axis_size("tensor")
    qkv_rows = (H + 2 * KV) * HD
    reach = (L_MAX + own - 2) // own
    reach += 1 - reach % 2
    window_rows = (reach + 1) * own
    chunk_rows = 2 * own if (reach + 1) % 2 == 0 else own
    tiles = (H + KV) * TILE
    f32, bf16 = jnp.float32, jnp.bfloat16
    shape = jax.ShapeDtypeStruct

    seq_ends = jnp.cumsum(seq_lengths)
    starts = seq_ends - seq_lengths
    first_place = lax.axis_index(AXES) * own
    places = first_place + jnp.arange(own, dtype=jnp.int32)
    begin = sequence_start(places, starts)
    first_key = first_place - reach * own
    low = jnp.tile(begin - first_key, GROUPS)[None, :]
    high = jnp.tile(places - first_key, GROUPS)[None, :]
    frequencies = jnp.power(ROPE_BASE, -2.0 * jnp.arange(HD // 2, dtype=f32) / HD)
    angles = (places - begin).astype(f32)[:, None] * frequencies[None, :]
    cosines, sines = jnp.cos(angles), jnp.sin(angles)
    zeros, ones = jnp.zeros((own, HD), f32), jnp.ones((own, HD), f32)
    cos_q = jnp.concatenate([cosines, cosines, zeros], axis=1)
    cos_kv = jnp.concatenate([cosines, cosines, ones], axis=1)
    sin_all = jnp.concatenate([-sines, sines, zeros], axis=1)

    gate_all = lax.all_gather(w_gate, "tensor", axis=0)
    up_all = lax.all_gather(w_up, "tensor", axis=0)
    down_all = lax.all_gather(w_down, "tensor", axis=0)
    w_out = jnp.pad(
        jnp.swapaxes(w_attn[:, qkv_rows:], 1, 2).reshape(layers, H, HD, width),
        ((0, 0), (0, 0), (HD, 0), (0, 0)),
    )

    stream = tokens.astype(f32)
    stored = []
    for layer in range(layers):
        queries, kv_own, normed = call(
            project_kernel,
            (
                shape((KV, GROUPS * own, TILE), bf16),
                shape((own, KV * TILE), bf16),
                shape((own, width), bf16),
            ),
            [pltpu.VMEM((tiles, width), bf16)],
            [whole_spec()] * 2 + [attn_spec(w_attn, layer)] + [whole_spec()] * 3,
        )(stream, attn_gain[layer][None], w_attn, cos_q, cos_kv, sin_all)
        window = call(
            functools.partial(fetch_kernel, count, reach),
            shape((reach + 1, own, KV * TILE), bf16),
            [pltpu.SemaphoreType.DMA((reach + 1,)) for _ in range(3)],
            collective_id=0,
            has_side_effects=True,
        )(kv_own).reshape(window_rows, KV * TILE)
        hidden_rows = gate_all.shape[0] * gate_all.shape[2]
        x_out, middle, normed_m, gate, up, hidden, mixed, lse = call(
            functools.partial(attend_kernel, chunk_rows),
            (
                shape((own, width), f32),
                shape((own, width), f32),
                shape((own, width), bf16),
                shape((own, hidden_rows), f32),
                shape((own, hidden_rows), f32),
                shape((own, hidden_rows), bf16),
                shape((KV, GROUPS * own, TILE), f32),
                shape((KV, 1, GROUPS * own), f32),
            ),
            [
                pltpu.VMEM((KV, TILE, GROUPS * own), f32),
                pltpu.VMEM((KV, 1, GROUPS * own), f32),
                pltpu.VMEM((KV, 1, GROUPS * own), f32),
            ],
            [whole_spec()] * 7 + [ffn_spec(gate_all, layer)] * 3,
        )(
            queries,
            window,
            low,
            high,
            stream,
            w_out[layer],
            mlp_gain[layer][None],
            gate_all,
            up_all,
            down_all,
        )
        stored.append((stream, queries, normed, window, middle, normed_m, gate, up, hidden, mixed, lse))
        stream = x_out

    upstream = cotangent
    gains = []
    parts = []
    for layer in reversed(range(layers)):
        x_in, queries, normed, window, middle, normed_m, gate, up, hidden, mixed, lse = stored[layer]
        hidden_rows = gate_all.shape[0] * gate_all.shape[2]
        gy, ggate, gup, gmid, go, gain_m = call(
            mlp_back_kernel,
            (
                shape((own, width), bf16),
                shape((own, hidden_rows), bf16),
                shape((own, hidden_rows), bf16),
                shape((own, width), f32),
                shape((own, width), bf16),
                shape((1, width), f32),
            ),
            (),
            [whole_spec()] * 5 + [ffn_spec(gate_all, layer)] * 3,
        )(
            upstream,
            middle,
            gate,
            up,
            mlp_gain[layer][None],
            gate_all,
            up_all,
            down_all,
        )
        heads = jnp.transpose(
            mixed.reshape(H, own, TILE)[:, :, HD:].astype(bf16), (1, 0, 2)
        ).reshape(own, H * HD)
        gq, gwin = call(
            functools.partial(attend_back_kernel, chunk_rows),
            (
                shape((KV, GROUPS * own, TILE), f32),
                shape((window_rows, KV * TILE), bf16),
            ),
            [
                pltpu.VMEM((KV, GROUPS * own, TILE), bf16),
                pltpu.VMEM((KV, 1, GROUPS * own), f32),
                pltpu.VMEM((KV, TILE, GROUPS * own), f32),
            ],
        )(go, w_out[layer], queries, window, low, high, mixed, lse)
        gkv = call(
            functools.partial(return_kernel, count, reach),
            shape((own, KV * TILE), f32),
            [
                pltpu.VMEM((reach // 2 + 1, own, KV * TILE), bf16),
                pltpu.VMEM((reach // 2, own, KV * TILE), bf16),
                pltpu.VMEM((reach // 2 + 1, own, KV * TILE), bf16),
            ]
            + [pltpu.SemaphoreType.DMA((reach + 1,)) for _ in range(4)],
            collective_id=1,
            has_side_effects=True,
        )(gwin.reshape(reach + 1, own, KV * TILE))
        gqkv, upstream, gain_a = call(
            project_back_kernel,
            (
                shape((own, tiles), bf16),
                shape((own, width), f32),
                shape((1, width), f32),
            ),
            [pltpu.VMEM((tiles, width), bf16)],
            [whole_spec()] * 5 + [attn_spec(w_attn, layer)] + [whole_spec()] * 3,
        )(gq, gkv, cos_q, cos_kv, sin_all, w_attn, x_in, attn_gain[layer][None], gmid)
        gains.append((gain_a, gain_m))

        parts.append([gqkv, normed, go, heads, ggate, gup, normed_m, hidden, gy])
    rows = [row for pair in gains[::-1] for row in pair]
    rows.append(jnp.zeros((-len(rows) % 8, width), f32))
    sums, gain_sums = sum_grads(parts[::-1], jnp.concatenate(rows, axis=0))
    attn_sum, gate_sum, up_sum, down_sum = [
        jnp.stack([entry[slot] for entry in sums], axis=0) for slot in range(4)
    ]
    gain_sums = gain_sums[: 2 * layers]
    return (
        stream,
        upstream,
        attn_sum,
        gain_sums[0::2],
        gate_sum,
        up_sum,
        down_sum,
        gain_sums[1::2],
    )


def solution(mesh):
    placed = (
        P(AXES, None),
        P(),
        P(),
        P(None, "tensor", None),
        P(None, "tensor", None),
        P(None, "tensor", None),
        P(),
        P(),
        P(AXES, None),
    )
    return jax.shard_map(
        body,
        mesh=mesh,
        in_specs=placed,
        out_specs=(
            P(AXES, None),
            P(AXES, None),
            P(None, AXES, None),
            P(),
            P(None, ("tensor", "dp"), None),
            P(None, ("tensor", "dp"), None),
            P(None, ("tensor", "dp"), None),
            P(),
        ),
        check_vma=False,
    )
```
